128 devices in a mesh: rows: 128 (over y, z, x, core).
Axes of the slice: x: 4, y: 4, z: 4, core: 2. Of those that a mesh axis runs over, the one named last changes fastest.
Arguments:
- users: float32 [262144, 128], P('rows'), may hold values from -2.5 to 2.5
- items: float32 [65536, 128], P('rows'), may hold values from -2.5 to 2.5
- ratings: bfloat16 [8192, 2, 256, 256], P('rows'), may hold values from -6 to 6
- observed: int32 [8192, 2, 8192], P('rows'), may hold values from 0 to 255
- tile_user: int32 [8192, 2], P('rows'), may hold values from 0 to 7
- fetch_owner: int32 [8192, 1], P('rows'), may hold values from 0 to 127, as said below
- fetch_block: int32 [8192], P('rows'), may hold values from 0 to 1
Outputs:
- new_users: float32 [262144, 128], P('rows')
- new_items: float32 [65536, 128], P('rows')
The draws below stay inside these ranges and needn't reach their ends.
Inputs may be any that keep to these rules, and one draw needn't show every extreme that they name: `fetch_owner`: within the 64 fetches of one device (aligned blocks of rows), no owner is named more than 1 times, and every device names some owner 1 times.
All inputs are finite; a program needn't handle non-finite values.
Results may differ from the reference program's by a relative error of at most 0.0041.
Values may be sent and summed in bfloat16 or wider, within the bound.
A program may use at most 256 MiB of HBM per device.

```python
import jax
import jax.numpy as jnp
from jax import lax

R = 128
BS = 256
UB_DEV = 8
IB_DEV = 2
FETCH_DEV = 64
TPF = 2
NU = 262144
NI = 65536
NFETCH = 8192
N_ROWS = 128


def draw_fetch_owner(key, part):
    key = jax.random.fold_in(key, 5)
    scores = jax.random.randint(key, (N_ROWS, N_ROWS), 0, 1048576, dtype=jnp.int32) * N_ROWS
    scores = scores + jnp.arange(N_ROWS, dtype=jnp.int32)[None, :]
    offset_ids = jnp.arange(N_ROWS, dtype=jnp.int32)[None, :]
    scores = jnp.where(offset_ids == N_ROWS // 2, -3, scores)
    scores = jnp.where(offset_ids == 1, -2, scores)
    scores = jnp.where(offset_ids == N_ROWS - 1, -1, scores)
    order = jnp.argsort(scores, axis=1, stable=True).astype(jnp.int32)
    position = jnp.arange(FETCH_DEV, dtype=jnp.int32) % N_ROWS
    offsets = jnp.take(order, position, axis=1)
    owners = (jnp.arange(N_ROWS, dtype=jnp.int32)[:, None] + offsets) % N_ROWS
    return owners.reshape(N_ROWS * FETCH_DEV, 1).astype(jnp.int32)


def draw_fetch_block(key, part):
    key = jax.random.fold_in(key, 7)
    first_key, second_key = jax.random.split(key)
    drawn = jax.random.randint(first_key, (N_ROWS, FETCH_DEV), 0, IB_DEV, dtype=jnp.int32)
    raised = 1 + jax.random.randint(second_key, (N_ROWS, FETCH_DEV), 0, IB_DEV - 1, dtype=jnp.int32)
    position = jnp.arange(FETCH_DEV, dtype=jnp.int32)[None, :]
    blocks = jnp.where(position < 3, raised, drawn)
    return blocks.reshape(N_ROWS * FETCH_DEV).astype(jnp.int32)


def place_ends(array, stream_key, low, largest):
    longest = array.shape.index(max(array.shape))
    spots = []
    for shift in (0, 1):
        where = [jax.random.randint(jax.random.fold_in(stream_key, axis), (), 0, length) for axis, length in enumerate(array.shape)]
        where[longest] = (where[longest] + shift) % array.shape[longest]
        spots.append(tuple(where))
    return array.at[spots[0]].set(low).at[spots[1]].set(largest)


def block_scale(rng, dims, cuts, low, top_value):
    def one(axis_at, blocks):
        heights = jax.random.uniform(jax.random.fold_in(jax.random.fold_in(rng, 6), axis_at), (blocks,), jnp.float32, low / len(cuts), top_value / len(cuts))
        return jnp.repeat(jnp.exp(heights), dims[axis_at] // blocks).reshape((-1,) + (1,) * (len(dims) - axis_at - 1))

    gain = one(*cuts[0])
    for cut in cuts[1:]:
        gain = gain * one(*cut)
    return gain


def gaussian(rng, extent, deviation, most, pieces=(), kind=jnp.bfloat16):
    values = jax.random.normal(rng, extent, jnp.float32) * deviation
    if len(pieces) > 0:
        values = block_scale(rng, extent, pieces, -0.22, 0.18) * values
    return jnp.clip(values, min=-most, max=most).astype(kind)


def setup_inputs(seed: int = 0) -> dict:
    key_list = jax.random.split(jax.random.key(seed), 8)
    users = gaussian(key_list[0], (NU, R), 0.3, 2.5, ((0, 128),), jnp.float32)
    items = gaussian(key_list[1], (NI, R), 0.3, 2.5, ((0, 128),), jnp.float32)
    ratings = gaussian(key_list[2], (NFETCH, TPF, BS, BS), 1.0, 6.0, ((0, 128),))
    observed = place_ends(jax.random.randint(key_list[3], (NFETCH, TPF, BS * BS // 8), 0, 256), jax.random.fold_in(key_list[3], 1), 0, 255).astype(jnp.int32)
    tile_user = place_ends(jax.random.randint(key_list[4], (NFETCH, TPF), 0, UB_DEV), jax.random.fold_in(key_list[4], 1), 0, UB_DEV - 1).astype(jnp.int32)
    fetch_owner = draw_fetch_owner(jax.random.fold_in(key_list[7], 71), 0)
    fetch_block = draw_fetch_block(jax.random.fold_in(key_list[7], 71), 0)
    return dict(users=users, items=items, ratings=ratings, observed=observed, tile_user=tile_user, fetch_owner=fetch_owner, fetch_block=fetch_block)


LEARN_RATE = 0.02


def unpack_bits(packed_pattern, width):
    shifts = jnp.arange(8, dtype=jnp.int32)
    leading = packed_pattern.shape[:-1]
    bits = jnp.right_shift(packed_pattern.reshape(leading + (width, width // 8, 1)), shifts) & 1
    return bits.reshape(leading + (width, width))


def reference(users, items, ratings, observed, tile_user, fetch_owner, fetch_block):
    item_blocks = items.astype(jnp.bfloat16).reshape(N_ROWS * IB_DEV, BS, R)
    user_blocks = users.astype(jnp.bfloat16).reshape(N_ROWS, UB_DEV, BS, R)
    highest = lax.Precision.HIGHEST

    def device_step(running_total, device_index):
        first_row = device_index * FETCH_DEV
        rating_rows = lax.dynamic_slice_in_dim(ratings, first_row, FETCH_DEV, 0)
        mask_rows = lax.dynamic_slice_in_dim(observed, first_row, FETCH_DEV, 0)
        chosen_ids = lax.dynamic_slice_in_dim(tile_user, first_row, FETCH_DEV, 0)
        owners = lax.dynamic_slice_in_dim(fetch_owner[:, 0], first_row, FETCH_DEV, 0)
        block_table = lax.dynamic_slice_in_dim(fetch_block, first_row, FETCH_DEV, 0)
        column = (owners * IB_DEV + block_table).astype(jnp.int32)
        fetched = jnp.take(item_blocks, column, axis=0).astype(jnp.float32)
        local_users = lax.dynamic_index_in_dim(user_blocks, device_index, 0, keepdims=False)
        chosen = jnp.take(local_users, chosen_ids, axis=0).astype(jnp.float32)
        mask_values = unpack_bits(mask_rows, BS).astype(jnp.float32)
        predicted = jnp.einsum("ftir,fjr->ftij", chosen, fetched, precision=highest)
        errors = (mask_values * (predicted - rating_rows.astype(jnp.float32))).astype(jnp.bfloat16)
        errors_wide = errors.astype(jnp.float32)
        partial_value = jnp.einsum("ftij,ftir->fjr", errors_wide, chosen, precision=highest).astype(jnp.bfloat16)
        terms = jnp.einsum("ftij,fjr->ftir", errors_wide, fetched, precision=highest)
        member = (chosen_ids[..., None] == jnp.arange(UB_DEV, dtype=jnp.int32)).astype(jnp.float32)
        user_part = jnp.einsum("ftir,ftu->uir", terms, member, precision=highest)
        running_total = running_total.at[column].add(partial_value.astype(jnp.float32))
        return running_total, user_part

    start = jnp.zeros((N_ROWS * IB_DEV, BS, R), jnp.float32)
    item_factor_gradient, user_grad = lax.scan(device_step, start, jnp.arange(N_ROWS, dtype=jnp.int32))
    new_users = users - LEARN_RATE * user_grad.reshape(users.shape)
    new_items = items - LEARN_RATE * item_factor_gradient.reshape(items.shape)
    return new_users, new_items
```

```python
import functools

import jax
import jax.numpy as jnp
from jax import lax
from jax.experimental import pallas as pl
from jax.experimental.pallas import tpu as pltpu
from jax.sharding import PartitionSpec as P

LEARN_RATE = 0.02
MESH = pl.DeviceIdType.MESH
R = 128
BS = 256
FETCHES = 64
ABSENT = 1e30

ORDERS = ((2, 0, 1), (0, 1, 2), (1, 2, 0))
GATHER_ROWS = ((0, 176), (176, 176), (352, 160))
REDUCE_ROWS = ((0, 96), (96, 80), (176, 80))


def position():
    me = lax.axis_index("rows")
    return (me // 32, (me // 8) % 4, (me // 2) % 4, me % 2)


def shifted(where, axis, step):
    y, z, x, core = [
        lax.rem(w + 4 + step, 4) if a == axis else w for a, w in enumerate(where[:3])
    ] + [where[3]]
    return ((y * 4 + z) * 4 + x) * 2 + core


def sibling(where):
    y, z, x, core = where
    return ((y * 4 + z) * 4 + x) * 2 + 1 - core


def greet(where):
    barrier = pltpu.get_barrier_semaphore()
    partners = [shifted(where, a, s) for a in range(3) for s in (1, -1, 2)] + [sibling(where)]
    for partner in partners:
        pl.semaphore_signal(barrier, inc=1, device_id=(partner,), device_id_type=MESH)
    pl.semaphore_wait(barrier, len(partners))


class Sender:
    def __init__(self, send_sems, recv_sems):
        self.send_sems, self.recv_sems, self.copies = send_sems, recv_sems, []

    def send(self, src, dst, device):
        n = len(self.copies)
        copy = pltpu.make_async_remote_copy(
            src_ref=src,
            dst_ref=dst,
            send_sem=self.send_sems.at[n],
            recv_sem=self.recv_sems.at[n],
            device_id=(device,),
            device_id_type=MESH,
        )
        copy.start()
        self.copies.append(copy)
        return copy

    def finish(self):
        for copy in self.copies:
            copy.wait_send()


GATHER_COPIES = 3 * (3 + 2 + 3 + 2 + 6 + 5) + 1 + 3 * (1 + 3 + 10 + 5)


def gather_kernel(
    items, ratings, observed, spread, bits, gathered, masked,
    own, words, rate_in, obs_in, rate_out, in_sems, out_sems, own_sem, send_sems, recv_sems,
):
    where = position()
    core = where[3]
    net = Sender(send_sems, recv_sems)

    def fetch_in(f, slot):
        return (
            pltpu.make_async_copy(ratings.at[f], rate_in.at[slot], in_sems.at[0, slot]),
            pltpu.make_async_copy(observed.at[f], obs_in.at[slot], in_sems.at[1, slot]),
        )

    def fetch_out(f, slot):
        return pltpu.make_async_copy(rate_out.at[slot], masked.at[f], out_sems.at[slot])

    for copy in fetch_in(0, 0):
        copy.start()

    def one(f, carry):
        slot = lax.rem(f, 2)

        @pl.when(f + 1 < FETCHES)
        def _():
            for copy in fetch_in(f + 1, 1 - slot):
                copy.start()

        for copy in fetch_in(f, slot):
            copy.wait()

        @pl.when(f >= 2)
        def _():
            fetch_out(f - 2, slot).wait()

        lane_group = lax.broadcasted_iota(jnp.int32, (64, 128), 1) // 32
        for t in range(2):
            packed = obs_in[slot, pl.ds(t, 64, stride=2), :].astype(jnp.float32)
            for quarter in range(4):
                words[t, pl.ds(quarter, 64, stride=4), :] = jnp.where(
                    lane_group == quarter, packed, 0.0
                )
            wide = jnp.dot(
                words[t].astype(jnp.bfloat16), spread[...], preferred_element_type=jnp.float32
            )
            seen = (wide.astype(jnp.int32) & bits[...]) != 0
            rate_out[slot, t] = jnp.where(
                seen, rate_in[slot, t].astype(jnp.float32), ABSENT
            ).astype(jnp.bfloat16)
        fetch_out(f, slot).start()
        return carry

    def work(first, last):
        lax.fori_loop(first, last, one, 0)

    def part(p, d1, d2, d3):
        a1, a2, a3 = ORDERS[p]
        index = [None] * 3
        index[a1], index[a2], index[a3] = d1, d2, d3
        return gathered.at[(core, *index, pl.ds(*GATHER_ROWS[p]))]

    every = slice(None)
    here = gathered.at[core, 0, 0, 0]
    own[...] = items[...].astype(jnp.bfloat16)
    place = pltpu.make_async_copy(own, here, own_sem)
    place.start()
    greet(where)

    first, line, plane, pair = {}, {}, {}, []
    twin = sibling(where)

    def mirror(p, d1, d2, d3):
        pair.append(net.send(part(p, d1, d2, d3), part(p, d1, d2, d3), twin))

    thirds = range(3)
    for p in thirds:
        a1, a2, a3 = ORDERS[p]
        mine = own.at[pl.ds(*GATHER_ROWS[p])]
        for s in (1, -1, 2):
            first[p, s] = net.send(mine, part(p, -s % 4, 0, 0), shifted(where, a1, s))
    for p in thirds:
        a1, a2, a3 = ORDERS[p]
        mine = own.at[pl.ds(*GATHER_ROWS[p])]
        for s in (1, -1):
            plane[p, 0, s] = net.send(mine, part(p, 0, 0, -s % 4), shifted(where, a3, s))
    pair.append(net.send(own, here, twin))
    place.wait()
    work(0, 4)
    groups = {0: (0, 0), 1: (slice(1, 4), 0), 2: (every, 3), 3: (every, 1), 4: (every, 2)}
    onward = {0: 1, 1: 1, 2: -1, 3: -1, 4: 1}

    def spread_group(p, g):
        a3 = ORDERS[p][2]
        d1, d2 = groups[g]
        for s in (1, -1):
            plane[p, g, s] = net.send(part(p, d1, d2, 0), part(p, d1, d2, -s % 4), shifted(where, a3, s))

    def pass_on(p, g):
        a3 = ORDERS[p][2]
        d1, d2 = groups[g]
        for s in (1, -1):
            plane[p, g, s].wait_recv()
            if onward[g] == s:
                plane[p, g, 2] = net.send(
                    part(p, d1, d2, -s % 4), part(p, d1, d2, 2), shifted(where, a3, s)
                )
            mirror(p, d1, d2, -s % 4)

    for p in thirds:
        a2 = ORDERS[p][1]
        for s in (1, -1, 2):
            first[p, s].wait_recv()
        for s in (1, -1, 2):
            line[p, s] = net.send(part(p, every, 0, 0), part(p, every, -s % 4, 0), shifted(where, a2, s))
    for p in thirds:
        spread_group(p, 1)
        mirror(p, slice(1, 4), 0, 0)
    work(4, 8)
    for p in thirds:
        pass_on(p, 0)
    work(8, 14)
    for g, s in ((2, 1), (3, -1), (4, 2)):
        for p in thirds:
            line[p, s].wait_recv()
            spread_group(p, g)
            mirror(p, every, -s % 4, 0)
        if g == 2:
            for p in thirds:
                pass_on(p, 1)
        work(14 + 6 * (g - 2), 20 + 6 * (g - 2))
    for g, upto in ((2, 42), (3, 52), (4, 64)):
        for p in thirds:
            pass_on(p, g)
        work({2: 32, 3: 42, 4: 52}[g], upto)
    for slot in range(2):
        fetch_out(FETCHES - 2 + slot, slot).wait()
    for g in groups:
        for p in thirds:
            plane[p, g, 2].wait_recv()
            mirror(p, *groups[g], 2)
    for copy in pair:
        copy.wait_recv()
    net.finish()


def gather(items, ratings, observed, spread, bits):
    return pl.pallas_call(
        gather_kernel,
        out_shape=(
            jax.ShapeDtypeStruct((2, 4, 4, 4, 512, R), jnp.bfloat16),
            jax.ShapeDtypeStruct(ratings.shape, jnp.bfloat16),
        ),
        in_specs=[
            pl.BlockSpec(memory_space=pltpu.VMEM),
            pl.BlockSpec(memory_space=pl.ANY),
            pl.BlockSpec(memory_space=pl.ANY),
            pl.BlockSpec(memory_space=pltpu.VMEM),
            pl.BlockSpec(memory_space=pltpu.VMEM),
        ],
        out_specs=[pl.BlockSpec(memory_space=pl.ANY)] * 2,
        scratch_shapes=[
            pltpu.VMEM((512, R), jnp.bfloat16),
            pltpu.VMEM((2, BS, 128), jnp.float32),
            pltpu.VMEM((2, 2, BS, BS), jnp.bfloat16),
            pltpu.VMEM((2, 128, 128), jnp.int32),
            pltpu.VMEM((2, 2, BS, BS), jnp.bfloat16),
            pltpu.SemaphoreType.DMA((2, 2)),
            pltpu.SemaphoreType.DMA((2,)),
            pltpu.SemaphoreType.DMA,
            pltpu.SemaphoreType.DMA((GATHER_COPIES,)),
            pltpu.SemaphoreType.DMA((GATHER_COPIES,)),
        ],
        compiler_params=pltpu.CompilerParams(
            collective_id=0, has_side_effects=True, vmem_limit_bytes=48 << 20
        ),
        name="gather_items",
    )(items, ratings, observed, spread, bits)


def tile_kernel(
    block_of, tile_user, owner, fetch_block, users, masked, fetched, new_users, partial, slots,
    user16, user16t,
):
    f = pl.program_id(0)

    @pl.when(f == 0)
    def _():
        def block(b, carry):
            rows = pl.ds(b * BS, BS)
            value = users[rows, :]
            user16[b] = value.astype(jnp.bfloat16)
            user16t[b] = value.T.astype(jnp.bfloat16)
            new_users[rows, :] = jnp.zeros((BS, R), jnp.float32)
            return carry

        lax.fori_loop(0, 8, block, 0)

        def clear(o, carry):
            slots[o] = -1
            return carry

        lax.fori_loop(0, 128, clear, 0)

        def note(g, carry):
            slots[owner[g]] = g * 2 + fetch_block[g]
            return carry

        lax.fori_loop(0, FETCHES, note, 0)

    item = fetched[0]
    total = jnp.zeros((R, BS), jnp.float32)
    for t in range(2):
        b = tile_user[f * 2 + t]
        predicted = lax.dot_general(
            user16[b], item, (((1,), (1,)), ((), ())), preferred_element_type=jnp.float32
        )
        miss = predicted - masked[0, t].astype(jnp.float32)
        error = jnp.where(miss > -0.5 * ABSENT, miss, 0.0).astype(jnp.bfloat16)
        total += jnp.dot(user16t[b], error, preferred_element_type=jnp.float32)
        rows = pl.ds(pl.multiple_of(b * BS, BS), BS)
        new_users[rows, :] += jnp.dot(error, item, preferred_element_type=jnp.float32)
    partial[0] = total.astype(jnp.bfloat16)

    @pl.when(f == FETCHES - 1)
    def _():
        def block(b, carry):
            rows = pl.ds(b * BS, BS)
            new_users[rows, :] = users[rows, :] - LEARN_RATE * new_users[rows, :]
            return carry

        lax.fori_loop(0, 8, block, 0)


def tiles(block_of, tile_user, owner, fetch_block, users, masked, fetched):
    return pl.pallas_call(
        tile_kernel,
        grid_spec=pltpu.PrefetchScalarGridSpec(
            num_scalar_prefetch=4,
            grid=(FETCHES,),
            in_specs=[
                pl.BlockSpec(users.shape, lambda f, *_: (0, 0)),
                pl.BlockSpec((1, 2, BS, BS), lambda f, *_: (f, 0, 0, 0)),
                pl.BlockSpec((1, BS, R), lambda f, block_of, *_: (block_of[f], 0, 0)),
            ],
            out_specs=[
                pl.BlockSpec(users.shape, lambda f, *_: (0, 0)),
                pl.BlockSpec((1, R, BS), lambda f, *_: (f, 0, 0)),
                pl.BlockSpec(memory_space=pltpu.SMEM),
            ],
            scratch_shapes=[
                pltpu.VMEM((8, BS, R), jnp.bfloat16),
                pltpu.VMEM((8, R, BS), jnp.bfloat16),
            ],
        ),
        out_shape=(
            jax.ShapeDtypeStruct(users.shape, jnp.float32),
            jax.ShapeDtypeStruct((FETCHES, R, BS), jnp.bfloat16),
            jax.ShapeDtypeStruct((128,), jnp.int32),
        ),
        compiler_params=pltpu.CompilerParams(vmem_limit_bytes=48 << 20),
        name="tile_gradients",
    )(block_of, tile_user, owner, fetch_block, users, masked, fetched)


REDUCE_COPIES = 48 + 3 * (4 + 4 + 4 + 3 + 3)


def reduce_kernel(
    slots, partial, items, new_items,
    parts, outgoing0, outgoing1, outgoing2, arriving0, arriving1, arriving2, dense0, dense1, dense2,
    far0, far1, far2, near0, near1, near2, plane0, plane1, plane2, line0, line1, line2,
    row0, row1, row2, unit0, unit1, unit2, grad, load_sem, send_sems, recv_sems,
):
    outgoing, arriving = (outgoing0, outgoing1, outgoing2), (arriving0, arriving1, arriving2)
    dense, far, near = (dense0, dense1, dense2), (far0, far1, far2), (near0, near1, near2)
    plane, line = (plane0, plane1, plane2), (line0, line1, line2)
    row, unit = (row0, row1, row2), (unit0, unit1, unit2)
    where = position()
    core = where[3]
    twin = sibling(where)
    load = pltpu.make_async_copy(partial, parts, load_sem)
    load.start()
    net = Sender(send_sems, recv_sems)
    greet(where)
    load.wait()
    thirds = range(3)

    def fill(target, p, parity, d3, d2):
        a1, a2, a3 = ORDERS[p]
        start, count = REDUCE_ROWS[p]

        def one(d1, carry):
            at = [None] * 3
            at[a1], at[a2], at[a3] = (
                lax.rem(where[a1] + d1, 4), lax.rem(where[a2] + d2, 4), lax.rem(where[a3] + d3, 4)
            )
            code = slots[((at[0] * 4 + at[1]) * 4 + at[2]) * 2 + parity]
            fetch = jnp.maximum(code, 0) // 2
            for block in range(2):
                low, high = max(start, block * R), min(start + count, (block + 1) * R)
                if low < high:
                    keep = (code >= 0) & (lax.rem(jnp.maximum(code, 0), 2) == block)
                    value = parts[fetch, pl.ds(low - block * R, high - low), :]
                    target[d3, d2, d1, pl.ds(low - start, high - low), :] = jnp.where(
                        keep, value, jnp.zeros_like(value)
                    )
            return carry

        lax.fori_loop(0, 4, one, 0)

    pair = {}

    def hand_over(d3, d2):
        for p in thirds:
            fill(outgoing[p], p, 1 - core, d3, d2)
            pair[p, d3, d2] = net.send(
                outgoing[p].at[d3, d2], arriving[p].at[d3, d2], twin
            )

    def collect(d3, d2):
        for p in thirds:
            fill(dense[p], p, core, d3, d2)
            pair[p, d3, d2].wait_recv()
            add_into(dense[p].at[d3, d2], arriving[p].at[d3, d2])

    def add_into(target, other):
        def one(n, carry):
            target[n] = (target[n].astype(jnp.float32) + other[n].astype(jnp.float32)).astype(
                jnp.bfloat16
            )
            return carry

        lax.fori_loop(0, 4, one, 0)

    via = {0: 1, 1: 1, 2: -1, 3: -1}
    relay, direct = {}, {}

    def send_far(d2):
        for p in thirds:
            s = via[d2]
            relay[p, d2] = net.send(
                dense[p].at[2, d2], far[p].at[d2], shifted(where, ORDERS[p][2], s)
            )

    def send_near(d2, s):
        for p in thirds:
            if via[d2] == s:
                relay[p, d2].wait_recv()
                add_into(dense[p].at[s % 4, d2], far[p].at[d2])
            direct[p, d2, s] = net.send(
                dense[p].at[s % 4, d2],
                near[p].at[0 if s == 1 else 1, d2],
                shifted(where, ORDERS[p][2], s),
            )

    todo = [(2, 0), (2, 2), (2, 1), (2, 3), (1, 2), (3, 0), (1, 3), (3, 1)]
    todo += [(1, 0), (3, 2), (1, 1), (3, 3), (0, 0), (0, 1), (0, 2), (0, 3)]
    ahead = 4
    for d3, d2 in todo[:ahead]:
        hand_over(d3, d2)
    for n, (d3, d2) in enumerate(todo):
        collect(d3, d2)
        if d3 == 2:
            send_far(d2)
        elif d3 != 0:
            send_near(d2, 1 if d3 == 1 else -1)
        if n + ahead < len(todo):
            hand_over(*todo[n + ahead])

    for d2 in (2, 1, 3, 0):
        for p in thirds:
            for s in (1, -1):
                direct[p, d2, s].wait_recv()

            def one(n, carry, p=p, d2=d2):
                total = dense[p][0, d2, n].astype(jnp.float32)
                total += near[p][0, d2, n].astype(jnp.float32)
                total += near[p][1, d2, n].astype(jnp.float32)
                plane[p][d2, n] = total.astype(jnp.bfloat16)
                return carry

            lax.fori_loop(0, 4, one, 0)
            if d2 != 0:
                s = {1: 1, 2: 2, 3: -1}[d2]
                direct[p, "line", s] = net.send(
                    plane[p].at[d2], line[p].at[d2 - 1], shifted(where, ORDERS[p][1], s)
                )
    for p in thirds:
        for s in (1, -1, 2):
            direct[p, "line", s].wait_recv()

        def one(n, carry, p=p):
            total = plane[p][0, n].astype(jnp.float32)
            for k in range(3):
                total += line[p][k, n].astype(jnp.float32)
            row[p][n] = total.astype(jnp.bfloat16)
            return carry

        lax.fori_loop(0, 4, one, 0)
        for d1, s in ((1, 1), (2, 2), (3, -1)):
            direct[p, "unit", s] = net.send(
                row[p].at[d1], unit[p].at[d1 - 1], shifted(where, ORDERS[p][0], s)
            )
    for p in thirds:
        start, count = REDUCE_ROWS[p]
        for s in (1, -1, 2):
            direct[p, "unit", s].wait_recv()
        total = row[p][0].astype(jnp.float32)
        for k in range(3):
            total += unit[p][k].astype(jnp.float32)
        grad[pl.ds(start, count), :] = total
    for block in range(2):
        rows = pl.ds(block * BS, BS)
        new_items[rows, :] = items[rows, :] - LEARN_RATE * grad[pl.ds(block * R, R), :].T
    net.finish()


def reduce_items(slots, partial, items):
    def each(*lead):
        return [pltpu.VMEM((*lead, count, BS), jnp.bfloat16) for _, count in REDUCE_ROWS]

    return pl.pallas_call(
        reduce_kernel,
        out_shape=jax.ShapeDtypeStruct(items.shape, jnp.float32),
        in_specs=[
            pl.BlockSpec(memory_space=pltpu.SMEM),
            pl.BlockSpec(memory_space=pl.ANY),
            pl.BlockSpec(memory_space=pltpu.VMEM),
        ],
        out_specs=pl.BlockSpec(memory_space=pltpu.VMEM),
        scratch_shapes=[
            pltpu.VMEM(partial.shape, jnp.bfloat16),
            *each(4, 4, 4),
            *each(4, 4, 4),
            *each(4, 4, 4),
            *each(4, 4),
            *each(2, 4, 4),
            *each(4, 4),
            *each(3, 4),
            *each(4),
            *each(3),
            pltpu.VMEM((BS, BS), jnp.float32),
            pltpu.SemaphoreType.DMA,
            pltpu.SemaphoreType.DMA((REDUCE_COPIES,)),
            pltpu.SemaphoreType.DMA((REDUCE_COPIES,)),
        ],
        compiler_params=pltpu.CompilerParams(
            collective_id=1, has_side_effects=True, vmem_limit_bytes=56 << 20
        ),
        name="reduce_items",
    )(slots, partial, items)


def body(users, items, ratings, observed, tile_user, fetch_owner, fetch_block):
    owner = fetch_owner[:, 0]
    chip = owner // 2
    mine = lax.axis_index("rows") // 2
    away = (
        (chip // 16 - mine // 16) % 4 * 16
        + (chip // 4 % 4 - mine // 4 % 4) % 4 * 4
        + (chip % 4 - mine % 4) % 4
    )
    block_of = ((owner % 2) * 64 + away) * 2 + fetch_block
    word = jnp.arange(128, dtype=jnp.int32)[:, None]
    column = jnp.arange(BS, dtype=jnp.int32)[None, :]
    spread = (word % 32 == column // 8).astype(jnp.bfloat16)
    bits = jnp.broadcast_to(jnp.left_shift(1, column % 8), (BS, BS))
    packed = observed.reshape(FETCHES, 2, 64, 128).transpose(0, 2, 1, 3).reshape(FETCHES, 128, 128)
    gathered, masked = gather(items, ratings, packed, spread, bits)
    new_users, partial, slots = tiles(
        block_of, tile_user.reshape(-1), owner, fetch_block, users, masked,
        gathered.reshape(256, BS, R),
    )
    new_items = reduce_items(slots, partial, items)
    return (new_users, new_items)


def solution(mesh):
    placed = (
        P("rows", None),
        P("rows", None),
        P("rows", None, None, None),
        P("rows", None, None),
        P("rows", None),
        P("rows", None),
        P("rows"),
    )
    return jax.shard_map(
        body,
        mesh=mesh,
        in_specs=placed,
        out_specs=(P("rows", None), P("rows", None)),
        check_vma=False,
    )
```

```python
import functools

import jax
import jax.numpy as jnp
from jax import lax
from jax.experimental import pallas as pl
from jax.experimental.pallas import tpu as pltpu
from jax.sharding import PartitionSpec as P

LEARN_RATE = 0.02
MESH = pl.DeviceIdType.MESH
R = 128
BS = 256
FETCHES = 64
CHUNK = 4
STEPS = FETCHES // CHUNK
ABSENT = 1e30

ORDERS = ((2, 0, 1), (0, 1, 2), (1, 2, 0))
GATHER_ROWS = ((0, 176), (176, 176), (352, 160))
REDUCE_ROWS = ((0, 96), (96, 80), (176, 80))


def position():
    me = lax.axis_index("rows")
    return (me // 32, (me // 8) % 4, (me // 2) % 4, me % 2)


def shifted(where, axis, step):
    y, z, x, core = [
        lax.rem(w + 4 + step, 4) if a == axis else w for a, w in enumerate(where[:3])
    ] + [where[3]]
    return ((y * 4 + z) * 4 + x) * 2 + core


def sibling(where):
    y, z, x, core = where
    return ((y * 4 + z) * 4 + x) * 2 + 1 - core


def greet(where):
    barrier = pltpu.get_barrier_semaphore()
    partners = [shifted(where, a, s) for a in range(3) for s in (1, -1, 2)] + [sibling(where)]
    for partner in partners:
        pl.semaphore_signal(barrier, inc=1, device_id=(partner,), device_id_type=MESH)
    pl.semaphore_wait(barrier, len(partners))


class Sender:
    def __init__(self, send_sems, recv_sems):
        self.send_sems, self.recv_sems, self.copies = send_sems, recv_sems, []

    def send(self, src, dst, device):
        n = len(self.copies)
        copy = pltpu.make_async_remote_copy(
            src_ref=src,
            dst_ref=dst,
            send_sem=self.send_sems.at[n],
            recv_sem=self.recv_sems.at[n],
            device_id=(device,),
            device_id_type=MESH,
        )
        copy.start()
        self.copies.append(copy)
        return copy

    def finish(self):
        for copy in self.copies:
            copy.wait_send()


GATHER_COPIES = 3 * (3 + 4 + 12 + 6) + 1 + 3 * (5 + 12 + 6)


def gather_kernel(
    items, ratings, observed, gathered, masked,
    spread, wide_own, own, words, rate_in, obs_in, rate_out, in_sems, out_sems, own_sem, send_sems, recv_sems,
):
    where = position()
    core = where[3]
    net = Sender(send_sems, recv_sems)

    def fetch_in(n, slot):
        some = pl.ds(n * CHUNK, CHUNK)
        return (
            pltpu.make_async_copy(ratings.at[some], rate_in.at[slot], in_sems.at[0, slot]),
            pltpu.make_async_copy(observed.at[some], obs_in.at[slot], in_sems.at[1, slot]),
        )

    def fetch_out(n, slot):
        return pltpu.make_async_copy(
            rate_out.at[slot], masked.at[pl.ds(n * CHUNK, CHUNK)], out_sems.at[slot]
        )

    def one(n, carry):
        slot = lax.rem(n, 2)

        @pl.when(n + 1 < STEPS)
        def _():
            for copy in fetch_in(n + 1, 1 - slot):
                copy.start()

        for copy in fetch_in(n, slot):
            copy.wait()

        @pl.when(n >= 2)
        def _():
            fetch_out(n - 2, slot).wait()

        lane_group = lax.broadcasted_iota(jnp.int32, (64, 128), 1) // 32
        bit = jnp.left_shift(1, lax.broadcasted_iota(jnp.int32, (1, BS), 1) % 8)

        def fetch(k, carry):
            for t in range(2):
                packed = obs_in[slot, k, pl.ds(t, 64, stride=2), :].astype(jnp.float32)
                for quarter in range(4):
                    words[t, pl.ds(quarter, 64, stride=4), :] = jnp.where(
                        lane_group == quarter, packed, 0.0
                    )
                wide = jnp.dot(
                    words[t].astype(jnp.bfloat16), spread[...], preferred_element_type=jnp.float32
                )
                seen = (wide.astype(jnp.int32) & bit) != 0
                rate_out[slot, k, t] = jnp.where(
                    seen, rate_in[slot, k, t].astype(jnp.float32), ABSENT
                ).astype(jnp.bfloat16)
            return carry

        lax.fori_loop(0, CHUNK, fetch, 0)
        fetch_out(n, slot).start()
        return carry

    def work(first, last):
        lax.fori_loop(first, last, one, 0)

    def part(p, d1, d2, d3):
        a1, a2, a3 = ORDERS[p]
        index = [None] * 3
        index[a1], index[a2], index[a3] = d1, d2, d3
        return gathered.at[(core, *index, pl.ds(*GATHER_ROWS[p]))]

    every = slice(None)
    here = gathered.at[core, 0, 0, 0]
    word = lax.broadcasted_iota(jnp.int32, (128, BS), 0)
    column = lax.broadcasted_iota(jnp.int32, (128, BS), 1)
    spread[...] = jnp.where(word % 32 == column // 8, 1.0, 0.0).astype(jnp.bfloat16)
    read = pltpu.make_async_copy(items, wide_own, own_sem)
    read.start()
    for copy in fetch_in(0, 0):
        copy.start()
    read.wait()
    own[...] = wide_own[...].astype(jnp.bfloat16)
    place = pltpu.make_async_copy(own, here, own_sem)
    place.start()
    greet(where)

    first, line, plane, pair = {}, {}, {}, []
    twin = sibling(where)

    def mirror(p, d1, d2, d3):
        pair.append(net.send(part(p, d1, d2, d3), part(p, d1, d2, d3), twin))

    thirds = range(3)
    for p in thirds:
        a1, a2, a3 = ORDERS[p]
        mine = own.at[pl.ds(*GATHER_ROWS[p])]
        for s in (1, -1, 2):
            first[p, s] = net.send(mine, part(p, -s % 4, 0, 0), shifted(where, a1, s))
    for p in thirds:
        a1, a2, a3 = ORDERS[p]
        mine = own.at[pl.ds(*GATHER_ROWS[p])]
        for s in (1, -1):
            plane[p, 0, s] = net.send(mine, part(p, 0, 0, -s % 4), shifted(where, a3, s))
    pair.append(net.send(own, here, twin))
    place.wait()
    work(0, 1)
    low, high = slice(0, 2), slice(2, 4)
    groups = {
        0: (0, 0), 1: (slice(1, 4), 0), 2: (every, 3), 3: (every, 1), 4: (low, 2), 5: (high, 2)
    }
    onward = {0: 1, 1: 1, 2: -1, 3: -1, 4: 1, 5: 1}

    def spread_group(p, g):
        a3 = ORDERS[p][2]
        d1, d2 = groups[g]
        for s in (1, -1):
            plane[p, g, s] = net.send(part(p, d1, d2, 0), part(p, d1, d2, -s % 4), shifted(where, a3, s))
        if g > 0:
            mirror(p, d1, d2, 0)

    def pass_on(g):
        for p in thirds:
            a3 = ORDERS[p][2]
            d1, d2 = groups[g]
            for s in (1, -1):
                plane[p, g, s].wait_recv()
                if onward[g] == s:
                    plane[p, g, 2] = net.send(
                        part(p, d1, d2, -s % 4), part(p, d1, d2, 2), shifted(where, a3, s)
                    )
                mirror(p, d1, d2, -s % 4)

    def passed(g):
        for p in thirds:
            plane[p, g, 2].wait_recv()
            mirror(p, *groups[g], 2)

    for p in thirds:
        a2 = ORDERS[p][1]
        for s in (1, -1, 2):
            first[p, s].wait_recv()
        for s in (1, -1):
            line[p, s] = net.send(part(p, every, 0, 0), part(p, every, -s % 4, 0), shifted(where, a2, s))
    for p in thirds:
        spread_group(p, 1)
    work(1, 2)
    pass_on(0)
    work(2, 3)
    for g, s, half in ((2, 1, low), (3, -1, high)):
        for p in thirds:
            line[p, s].wait_recv()
            line[p, g + 2] = net.send(
                part(p, half, -s % 4, 0), part(p, half, 2, 0), shifted(where, ORDERS[p][1], s)
            )
            spread_group(p, g)
    work(3, 5)
    pass_on(1)
    work(5, 7)
    for g, half in ((4, low), (5, high)):
        for p in thirds:
            line[p, g].wait_recv()
            spread_group(p, g)
    work(7, 9)
    pass_on(2)
    passed(0)
    work(9, 11)
    pass_on(3)
    passed(1)
    work(11, 13)
    pass_on(4)
    work(13, 14)
    pass_on(5)
    work(14, STEPS)
    passed(2)
    passed(3)
    for slot in range(2):
        fetch_out(STEPS - 2 + slot, slot).wait()
    passed(4)
    passed(5)
    for copy in pair:
        copy.wait_recv()
    net.finish()


def gather(items, ratings, observed):
    return pl.pallas_call(
        gather_kernel,
        out_shape=(
            jax.ShapeDtypeStruct((2, 4, 4, 4, 512, R), jnp.bfloat16),
            jax.ShapeDtypeStruct(ratings.shape, jnp.bfloat16),
        ),
        in_specs=[
            pl.BlockSpec(memory_space=pltpu.HBM),
            pl.BlockSpec(memory_space=pltpu.HBM),
            pl.BlockSpec(memory_space=pltpu.HBM),
        ],
        out_specs=[pl.BlockSpec(memory_space=pltpu.HBM)] * 2,
        scratch_shapes=[
            pltpu.VMEM((128, BS), jnp.bfloat16),
            pltpu.VMEM((512, R), jnp.float32),
            pltpu.VMEM((512, R), jnp.bfloat16),
            pltpu.VMEM((2, BS, 128), jnp.float32),
            pltpu.VMEM((2, CHUNK, 2, BS, BS), jnp.bfloat16),
            pltpu.VMEM((2, CHUNK, 128, 128), jnp.int32),
            pltpu.VMEM((2, CHUNK, 2, BS, BS), jnp.bfloat16),
            pltpu.SemaphoreType.DMA((2, 2)),
            pltpu.SemaphoreType.DMA((2,)),
            pltpu.SemaphoreType.DMA,
            pltpu.SemaphoreType.DMA((GATHER_COPIES,)),
            pltpu.SemaphoreType.DMA((GATHER_COPIES,)),
        ],
        compiler_params=pltpu.CompilerParams(
            collective_id=0, has_side_effects=True, vmem_limit_bytes=60 << 20
        ),
        name="gather_items",
    )(items, ratings, observed)


GROUP = 8


def tile_kernel(tile_user, owner, fetch_block, users, masked, *rest):
    fetched = rest[:GROUP]
    new_users, partial, slots, user16, user16t, errors = rest[GROUP:]
    g = pl.program_id(0)

    @pl.when(g == 0)
    def _():
        def block(b, carry):
            rows = pl.ds(b * BS, BS)
            value = users[rows, :]
            user16[b] = value.astype(jnp.bfloat16)
            user16t[b] = value.T.astype(jnp.bfloat16)
            new_users[rows, :] = jnp.zeros((BS, R), jnp.float32)
            return carry

        lax.fori_loop(0, 8, block, 0)

        def clear(o, carry):
            slots[o] = -1
            return carry

        lax.fori_loop(0, 128, clear, 0)

        def note(f, carry):
            slots[owner[f]] = f * 2 + fetch_block[f]
            return carry

        lax.fori_loop(0, FETCHES, note, 0)

    which = [[tile_user[t, g * GROUP + k] for t in range(2)] for k in range(GROUP)]
    for k in range(GROUP):
        for t in range(2):
            predicted = lax.dot_general(
                user16[which[k][t]], fetched[k][0], (((1,), (1,)), ((), ())),
                preferred_element_type=jnp.float32,
            )
            miss = predicted - masked[k, t].astype(jnp.float32)
            errors[k, t] = jnp.where(miss > -0.5 * ABSENT, miss, 0.0).astype(jnp.bfloat16)
    for k in range(GROUP):
        total = jnp.zeros((R, BS), jnp.float32)
        for t in range(2):
            total += jnp.dot(
                user16t[which[k][t]], errors[k, t], preferred_element_type=jnp.float32
            )
        partial[k] = total.astype(jnp.bfloat16)
    for k in range(GROUP):
        for t in range(2):
            rows = pl.ds(pl.multiple_of(which[k][t] * BS, BS), BS)
            new_users[rows, :] += jnp.dot(
                errors[k, t], fetched[k][0], preferred_element_type=jnp.float32
            )

    @pl.when(g == pl.num_programs(0) - 1)
    def _():
        def block(b, carry):
            rows = pl.ds(b * BS, BS)
            new_users[rows, :] = users[rows, :] - LEARN_RATE * new_users[rows, :]
            return carry

        lax.fori_loop(0, 8, block, 0)


def tiles(tile_user, owner, fetch_block, users, masked, fetched):
    def item(k):
        def place(g, tile_user, owner, fetch_block):
            f = g * GROUP + k
            chip, mine = owner[f] // 2, lax.axis_index("rows") // 2
            away = (
                lax.rem(chip // 16 + 4 - mine // 16, 4) * 16
                + lax.rem(lax.rem(chip // 4, 4) + 4 - lax.rem(mine // 4, 4), 4) * 4
                + lax.rem(lax.rem(chip, 4) + 4 - lax.rem(mine, 4), 4)
            )
            return (lax.rem(owner[f], 2) * 64 + away) * 2 + fetch_block[f], 0, 0

        return pl.BlockSpec((1, BS, R), place)

    return pl.pallas_call(
        tile_kernel,
        grid_spec=pltpu.PrefetchScalarGridSpec(
            num_scalar_prefetch=3,
            grid=(FETCHES // GROUP,),
            in_specs=[
                pl.BlockSpec(users.shape, lambda g, *_: (0, 0)),
                pl.BlockSpec((GROUP, 2, BS, BS), lambda g, *_: (g, 0, 0, 0)),
                *[item(k) for k in range(GROUP)],
            ],
            out_specs=[
                pl.BlockSpec(users.shape, lambda g, *_: (0, 0)),
                pl.BlockSpec((GROUP, R, BS), lambda g, *_: (g, 0, 0)),
                pl.BlockSpec(memory_space=pltpu.SMEM),
            ],
            scratch_shapes=[
                pltpu.VMEM((8, BS, R), jnp.bfloat16),
                pltpu.VMEM((8, R, BS), jnp.bfloat16),
                pltpu.VMEM((GROUP, 2, BS, BS), jnp.bfloat16),
            ],
        ),
        out_shape=(
            jax.ShapeDtypeStruct(users.shape, jnp.float32),
            jax.ShapeDtypeStruct((FETCHES, R, BS), jnp.bfloat16),
            jax.ShapeDtypeStruct((128,), jnp.int32),
        ),
        compiler_params=pltpu.CompilerParams(vmem_limit_bytes=48 << 20),
        name="tile_gradients",
    )(tile_user, owner, fetch_block, users, masked, *([fetched] * GROUP))


REDUCE_COPIES = 48 + 3 * (4 + 4 + 4 + 3 + 3)


def reduce_kernel(
    slots, parts, item_grad,
    outgoing0, outgoing1, outgoing2, arriving0, arriving1, arriving2, dense0, dense1, dense2,
    far0, far1, far2, near0, near1, near2, plane0, plane1, plane2, line0, line1, line2,
    row0, row1, row2, unit0, unit1, unit2, grad, send_sems, recv_sems,
):
    outgoing, arriving = (outgoing0, outgoing1, outgoing2), (arriving0, arriving1, arriving2)
    dense, far, near = (dense0, dense1, dense2), (far0, far1, far2), (near0, near1, near2)
    plane, line = (plane0, plane1, plane2), (line0, line1, line2)
    row, unit = (row0, row1, row2), (unit0, unit1, unit2)
    where = position()
    core = where[3]
    twin = sibling(where)
    net = Sender(send_sems, recv_sems)
    greet(where)
    thirds = range(3)

    def fill(target, p, parity, d3, d2):
        a1, a2, a3 = ORDERS[p]
        start, count = REDUCE_ROWS[p]

        def one(d1, carry):
            at = [None] * 3
            at[a1], at[a2], at[a3] = (
                lax.rem(where[a1] + d1, 4), lax.rem(where[a2] + d2, 4), lax.rem(where[a3] + d3, 4)
            )
            code = slots[((at[0] * 4 + at[1]) * 4 + at[2]) * 2 + parity]
            fetch = jnp.maximum(code, 0) // 2
            for block in range(2):
                low, high = max(start, block * R), min(start + count, (block + 1) * R)
                if low < high:
                    keep = (code >= 0) & (lax.rem(jnp.maximum(code, 0), 2) == block)
                    value = parts[fetch, pl.ds(low - block * R, high - low), :]
                    target[d3, d2, d1, pl.ds(low - start, high - low), :] = jnp.where(
                        keep, value, jnp.zeros_like(value)
                    )
            return carry

        lax.fori_loop(0, 4, one, 0)

    pair = {}

    def hand_over(d3, d2):
        for p in thirds:
            fill(outgoing[p], p, 1 - core, d3, d2)
            pair[p, d3, d2] = net.send(
                outgoing[p].at[d3, d2], arriving[p].at[d3, d2], twin
            )

    def collect(d3, d2):
        for p in thirds:
            fill(dense[p], p, core, d3, d2)
            pair[p, d3, d2].wait_recv()
            add_into(dense[p].at[d3, d2], arriving[p].at[d3, d2])

    def add_into(target, other):
        def one(n, carry):
            target[n] = (target[n].astype(jnp.float32) + other[n].astype(jnp.float32)).astype(
                jnp.bfloat16
            )
            return carry

        lax.fori_loop(0, 4, one, 0)

    via = {0: 1, 1: 1, 2: -1, 3: -1}
    relay, direct = {}, {}

    def send_far(d2):
        for p in thirds:
            s = via[d2]
            relay[p, d2] = net.send(
                dense[p].at[2, d2], far[p].at[d2], shifted(where, ORDERS[p][2], s)
            )

    def send_near(d2, s):
        for p in thirds:
            if via[d2] == s:
                relay[p, d2].wait_recv()
                add_into(dense[p].at[s % 4, d2], far[p].at[d2])
            direct[p, d2, s] = net.send(
                dense[p].at[s % 4, d2],
                near[p].at[0 if s == 1 else 1, d2],
                shifted(where, ORDERS[p][2], s),
            )

    todo = [(2, 0), (2, 2), (2, 1), (2, 3), (1, 2), (3, 0), (1, 3), (3, 1)]
    todo += [(1, 0), (3, 2), (1, 1), (3, 3), (0, 0), (0, 1), (0, 2), (0, 3)]
    ahead = 4
    for d3, d2 in todo[:ahead]:
        hand_over(d3, d2)
    for n, (d3, d2) in enumerate(todo):
        collect(d3, d2)
        if d3 == 2:
            send_far(d2)
        elif d3 != 0:
            send_near(d2, 1 if d3 == 1 else -1)
        if n + ahead < len(todo):
            hand_over(*todo[n + ahead])

    for d2 in (2, 1, 3, 0):
        for p in thirds:
            for s in (1, -1):
                direct[p, d2, s].wait_recv()

            def one(n, carry, p=p, d2=d2):
                total = dense[p][0, d2, n].astype(jnp.float32)
                total += near[p][0, d2, n].astype(jnp.float32)
                total += near[p][1, d2, n].astype(jnp.float32)
                plane[p][d2, n] = total.astype(jnp.bfloat16)
                return carry

            lax.fori_loop(0, 4, one, 0)
            if d2 != 0:
                s = {1: 1, 2: 2, 3: -1}[d2]
                direct[p, "line", s] = net.send(
                    plane[p].at[d2], line[p].at[d2 - 1], shifted(where, ORDERS[p][1], s)
                )
    for p in thirds:
        for s in (1, -1, 2):
            direct[p, "line", s].wait_recv()

        def one(n, carry, p=p):
            total = plane[p][0, n].astype(jnp.float32)
            for k in range(3):
                total += line[p][k, n].astype(jnp.float32)
            row[p][n] = total.astype(jnp.bfloat16)
            return carry

        lax.fori_loop(0, 4, one, 0)
        for d1, s in ((1, 1), (2, 2), (3, -1)):
            direct[p, "unit", s] = net.send(
                row[p].at[d1], unit[p].at[d1 - 1], shifted(where, ORDERS[p][0], s)
            )
    for p in thirds:
        start, count = REDUCE_ROWS[p]
        for s in (1, -1, 2):
            direct[p, "unit", s].wait_recv()
        total = row[p][0].astype(jnp.float32)
        for k in range(3):
            total += unit[p][k].astype(jnp.float32)
        grad[pl.ds(start, count), :] = total
    for block in range(2):
        rows = pl.ds(block * BS, BS)
        item_grad[rows, :] = grad[pl.ds(block * R, R), :].T
    net.finish()


def reduce_items(slots, partial):
    def each(*lead):
        return [pltpu.VMEM((*lead, count, BS), jnp.bfloat16) for _, count in REDUCE_ROWS]

    return pl.pallas_call(
        reduce_kernel,
        out_shape=jax.ShapeDtypeStruct((2 * BS, R), jnp.float32),
        in_specs=[
            pl.BlockSpec(memory_space=pltpu.SMEM),
            pl.BlockSpec(memory_space=pltpu.VMEM),
        ],
        out_specs=pl.BlockSpec(memory_space=pltpu.VMEM),
        scratch_shapes=[
            *each(4, 4, 4),
            *each(4, 4, 4),
            *each(4, 4, 4),
            *each(4, 4),
            *each(2, 4, 4),
            *each(4, 4),
            *each(3, 4),
            *each(4),
            *each(3),
            pltpu.VMEM((BS, BS), jnp.float32),
            pltpu.SemaphoreType.DMA((REDUCE_COPIES,)),
            pltpu.SemaphoreType.DMA((REDUCE_COPIES,)),
        ],
        compiler_params=pltpu.CompilerParams(
            collective_id=1, has_side_effects=True, vmem_limit_bytes=44 << 20
        ),
        name="reduce_items",
    )(slots, partial)


def body(users, items, ratings, observed, tile_user, fetch_owner, fetch_block):
    owner = fetch_owner[:, 0]
    packed = observed.reshape(FETCHES, 2, 64, 128).transpose(0, 2, 1, 3).reshape(FETCHES, 128, 128)
    gathered, masked = gather(items, ratings, packed)
    new_users, partial, slots = tiles(
        tile_user.T, owner, fetch_block, users, masked,
        gathered.reshape(256, BS, R),
    )
    new_items = items - LEARN_RATE * reduce_items(slots, partial)
    return (new_users, new_items)


def solution(mesh):
    placed = (
        P("rows", None),
        P("rows", None),
        P("rows", None, None, None),
        P("rows", None, None),
        P("rows", None),
        P("rows", None),
        P("rows"),
    )
    return jax.shard_map(
        body,
        mesh=mesh,
        in_specs=placed,
        out_specs=(P("rows", None), P("rows", None)),
        check_vma=False,
    )
```

```python
import functools

import jax
import jax.numpy as jnp
from jax import lax
from jax.experimental import pallas as pl
from jax.experimental.pallas import tpu as pltpu
from jax.sharding import PartitionSpec as P

LEARN_RATE = 0.02
MESH = pl.DeviceIdType.MESH
in_space = pltpu.with_memory_space_constraint
R = 128
BS = 256
FETCHES = 64
CHUNK = 4
STEPS = FETCHES // CHUNK
ABSENT = 1e30

ORDERS = ((2, 0, 1), (0, 1, 2), (1, 2, 0))
GATHER_ROWS = ((0, 176), (176, 176), (352, 160))
REDUCE_ROWS = ((0, 96), (96, 80), (176, 80))


def position():
    me = lax.axis_index("rows")
    return (me // 32, (me // 8) % 4, (me // 2) % 4, me % 2)


def shifted(where, axis, step):
    y, z, x, core = [
        lax.rem(w + 4 + step, 4) if a == axis else w for a, w in enumerate(where[:3])
    ] + [where[3]]
    return ((y * 4 + z) * 4 + x) * 2 + core


def sibling(where):
    y, z, x, core = where
    return ((y * 4 + z) * 4 + x) * 2 + 1 - core


def greet(where):
    barrier = pltpu.get_barrier_semaphore()
    partners = [shifted(where, a, s) for a in range(3) for s in (1, -1, 2)] + [sibling(where)]
    for partner in partners:
        pl.semaphore_signal(barrier, inc=1, device_id=(partner,), device_id_type=MESH)
    return lambda: pl.semaphore_wait(barrier, len(partners))


class Sender:
    def __init__(self, send_sems, recv_sems):
        self.send_sems, self.recv_sems, self.copies = send_sems, recv_sems, []

    def send(self, src, dst, device):
        n = len(self.copies)
        copy = pltpu.make_async_remote_copy(
            src_ref=src,
            dst_ref=dst,
            send_sem=self.send_sems.at[n],
            recv_sem=self.recv_sems.at[n],
            device_id=(device,),
            device_id_type=MESH,
        )
        copy.start()
        self.copies.append(copy)
        return copy

    def finish(self):
        for copy in self.copies:
            copy.wait_send()


GATHER_COPIES = 3 * (3 + 4 + 14 + 7) + 1 + 3 * (6 + 14 + 7)


def gather_kernel(
    items, ratings, observed, users, gathered, masked, user16, user16t,
    spread, wide_own, own, words, rate_in, obs_in, wide_users, in_sems, own_sem, user_sem, send_sems, recv_sems,
):
    where = position()
    core = where[3]
    net = Sender(send_sems, recv_sems)

    def fetch_in(n, slot):
        some = pl.ds(n * CHUNK, CHUNK)
        return (
            pltpu.make_async_copy(ratings.at[some], rate_in.at[slot], in_sems.at[0, slot]),
            pltpu.make_async_copy(observed.at[some], obs_in.at[slot], in_sems.at[1, slot]),
        )

    def one(n, carry):
        slot = lax.rem(n, 2)

        @pl.when(n + 1 < STEPS)
        def _():
            for copy in fetch_in(n + 1, 1 - slot):
                copy.start()

        for copy in fetch_in(n, slot):
            copy.wait()

        lane_group = lax.broadcasted_iota(jnp.int32, (64, 128), 1) // 32
        bit = jnp.left_shift(1, lax.broadcasted_iota(jnp.int32, (1, BS), 1) % 8)

        def fetch(k, carry):
            for t in range(2):
                packed = obs_in[slot, k, pl.ds(t, 64, stride=2), :].astype(jnp.float32)
                for quarter in range(4):
                    words[t, pl.ds(quarter, 64, stride=4), :] = jnp.where(
                        lane_group == quarter, packed, 0.0
                    )
                wide = jnp.dot(
                    words[t].astype(jnp.bfloat16), spread[...], preferred_element_type=jnp.float32
                )
                seen = (wide.astype(jnp.int32) & bit) != 0
                masked[n * CHUNK + k, t] = jnp.where(
                    seen, rate_in[slot, k, t].astype(jnp.float32), ABSENT
                ).astype(jnp.bfloat16)
            return carry

        lax.fori_loop(0, CHUNK, fetch, 0)
        return carry

    def work(first, last):
        lax.fori_loop(first, last, one, 0)

    def part(p, d1, d2, d3):
        a1, a2, a3 = ORDERS[p]
        index = [None] * 3
        index[a1], index[a2], index[a3] = d1, d2, d3
        return gathered.at[(core, *index, pl.ds(*GATHER_ROWS[p]))]

    every = slice(None)
    here = gathered.at[core, 0, 0, 0]
    greeted = greet(where)
    read = pltpu.make_async_copy(items, wide_own, own_sem)
    read.start()
    for copy in fetch_in(0, 0):
        copy.start()
    read_users = pltpu.make_async_copy(users, wide_users, user_sem)
    read_users.start()
    word = lax.broadcasted_iota(jnp.int32, (128, BS), 0)
    column = lax.broadcasted_iota(jnp.int32, (128, BS), 1)
    spread[...] = jnp.where(word % 32 == column // 8, 1.0, 0.0).astype(jnp.bfloat16)
    read.wait()
    own[...] = wide_own[...].astype(jnp.bfloat16)
    place = pltpu.make_async_copy(own, here, own_sem)
    place.start()
    greeted()

    first, line, plane, pair = {}, {}, {}, []
    twin = sibling(where)

    def mirror(p, d1, d2, d3):
        pair.append(net.send(part(p, d1, d2, d3), part(p, d1, d2, d3), twin))

    thirds = range(3)
    for p in thirds:
        a1, a2, a3 = ORDERS[p]
        mine = own.at[pl.ds(*GATHER_ROWS[p])]
        for s in (1, -1, 2):
            first[p, s] = net.send(mine, part(p, -s % 4, 0, 0), shifted(where, a1, s))
    for p in thirds:
        a1, a2, a3 = ORDERS[p]
        mine = own.at[pl.ds(*GATHER_ROWS[p])]
        for s in (1, -1):
            plane[p, 0, s] = net.send(mine, part(p, 0, 0, -s % 4), shifted(where, a3, s))
    pair.append(net.send(own, here, twin))
    def halve(b, carry):
        value = wide_users[pl.ds(b * BS, BS), :]
        user16[b] = value.astype(jnp.bfloat16)
        user16t[b] = value.T.astype(jnp.bfloat16)
        return carry

    place.wait()
    work(0, 1)
    low, high = slice(0, 2), slice(2, 4)
    groups = {
        0: (0, 0), 1: (slice(1, 4), 0), 2: (every, 3), 3: (low, 1), 6: (high, 1),
        4: (low, 2), 5: (high, 2),
    }
    onward = {0: 1, 1: 1, 2: -1, 3: -1, 6: -1, 4: 1, 5: 1}

    def spread_group(p, g):
        a3 = ORDERS[p][2]
        d1, d2 = groups[g]
        for s in (1, -1):
            plane[p, g, s] = net.send(part(p, d1, d2, 0), part(p, d1, d2, -s % 4), shifted(where, a3, s))
        if g > 0:
            mirror(p, d1, d2, 0)

    def pass_on(g):
        for p in thirds:
            a3 = ORDERS[p][2]
            d1, d2 = groups[g]
            for s in (1, -1):
                plane[p, g, s].wait_recv()
                if onward[g] == s:
                    plane[p, g, 2] = net.send(
                        part(p, d1, d2, -s % 4), part(p, d1, d2, 2), shifted(where, a3, s)
                    )
                mirror(p, d1, d2, -s % 4)

    def passed(g):
        for p in thirds:
            plane[p, g, 2].wait_recv()
            mirror(p, *groups[g], 2)

    for p in thirds:
        a2 = ORDERS[p][1]
        for s in (1, -1, 2):
            first[p, s].wait_recv()
        for s in (1, -1):
            line[p, s] = net.send(part(p, every, 0, 0), part(p, every, -s % 4, 0), shifted(where, a2, s))
    for p in thirds:
        spread_group(p, 1)
    work(1, 2)
    pass_on(0)
    read_users.wait()
    lax.fori_loop(0, 8, halve, 0)
    work(2, 3)
    for g, s, half in ((2, 1, low), (3, -1, high)):
        for p in thirds:
            line[p, s].wait_recv()
            line[p, g + 2] = net.send(
                part(p, half, -s % 4, 0), part(p, half, 2, 0), shifted(where, ORDERS[p][1], s)
            )
            spread_group(p, g)
            if g == 3:
                spread_group(p, 6)
    work(3, 5)
    pass_on(1)
    work(5, 7)
    for g, half in ((4, low), (5, high)):
        for p in thirds:
            line[p, g].wait_recv()
            spread_group(p, g)
    work(7, 9)
    pass_on(2)
    passed(0)
    work(9, 11)
    pass_on(3)
    pass_on(6)
    passed(1)
    work(11, 13)
    pass_on(4)
    work(13, 14)
    pass_on(5)
    work(14, STEPS)
    passed(2)
    passed(4)
    passed(3)
    passed(5)
    passed(6)
    for copy in pair:
        copy.wait_recv()
    net.finish()


def gather(items, ratings, observed, users):
    return pl.pallas_call(
        gather_kernel,
        out_shape=(
            pltpu.HBM((2, 4, 4, 4, 512, R), jnp.bfloat16),
            pltpu.VMEM(ratings.shape, jnp.bfloat16),
            pltpu.VMEM((8, BS, R), jnp.bfloat16),
            pltpu.VMEM((8, R, BS), jnp.bfloat16),
        ),
        in_specs=[pl.BlockSpec(memory_space=pltpu.HBM)] * 4,
        out_specs=[pl.BlockSpec(memory_space=pltpu.HBM)]
        + [pl.BlockSpec(memory_space=pltpu.VMEM)] * 3,
        scratch_shapes=[
            pltpu.VMEM((128, BS), jnp.bfloat16),
            pltpu.VMEM((512, R), jnp.float32),
            pltpu.VMEM((512, R), jnp.bfloat16),
            pltpu.VMEM((2, BS, 128), jnp.float32),
            pltpu.VMEM((2, CHUNK, 2, BS, BS), jnp.bfloat16),
            pltpu.VMEM((2, CHUNK, 128, 128), jnp.int32),
            pltpu.VMEM(users.shape, jnp.float32),
            pltpu.SemaphoreType.DMA((2, 2)),
            pltpu.SemaphoreType.DMA,
            pltpu.SemaphoreType.DMA,
            pltpu.SemaphoreType.DMA((GATHER_COPIES,)),
            pltpu.SemaphoreType.DMA((GATHER_COPIES,)),
        ],
        compiler_params=pltpu.CompilerParams(
            collective_id=0, has_side_effects=True, vmem_limit_bytes=12 << 20
        ),
        name="gather_items",
    )(*[in_space(x, pltpu.HBM) for x in (items, ratings, observed, users)])


GROUP = 8
GROUPS = FETCHES // GROUP


def tile_kernel(
    tile_user, owner, fetch_block, users, user16, user16t, masked, fetched,
    new_users, partial, slots, blocks, errors, grad, in_sems, out_sems,
):
    where = position()

    def read(f):
        chip = owner[f] // 2
        at = (chip // 16, lax.rem(chip // 4, 4), lax.rem(chip, 4))
        dy, dz, dx = [lax.rem(a + 4 - w, 4) for a, w in zip(at, where)]
        away = ((lax.rem(owner[f], 2) * 4 + dy) * 4 + dz) * 4 + dx
        return pltpu.make_async_copy(
            fetched.at[away * 2 + fetch_block[f]], blocks.at[f], in_sems.at[f]
        )

    def write(b):
        rows = pl.ds(b * BS, BS)
        return pltpu.make_async_copy(grad.at[rows], new_users.at[rows], out_sems.at[b])

    for f in range(2 * GROUP):
        read(f).start()
    grad[...] = jnp.zeros_like(grad)

    def one(g, carry):
        @pl.when(g + 2 < GROUPS)
        def _():
            for k in range(GROUP):
                read((g + 2) * GROUP + k).start()

        @pl.when(g < GROUPS // 2)
        def _():
            for k in range(32):
                slots[g * 32 + k] = -1

        @pl.when(g >= GROUPS // 2)
        def _():
            for k in range(16):
                f = (g - GROUPS // 2) * 16 + k
                slots[owner[f]] = f * 2 + fetch_block[f]

        fetches = [g * GROUP + k for k in range(GROUP)]
        which = [[tile_user[t, f] for t in range(2)] for f in fetches]
        for f in fetches:
            pltpu.make_async_copy(fetched.at[0], blocks.at[f], in_sems.at[f]).wait()
        for k, f in enumerate(fetches):
            for t in range(2):
                predicted = lax.dot_general(
                    user16[which[k][t]], blocks[f], (((1,), (1,)), ((), ())),
                    preferred_element_type=jnp.float32,
                )
                miss = predicted - masked[f, t].astype(jnp.float32)
                errors[k, t] = jnp.where(miss > -0.5 * ABSENT, miss, 0.0).astype(jnp.bfloat16)
        for k, f in enumerate(fetches):
            total = jnp.zeros((R, BS), jnp.float32)
            for t in range(2):
                total += jnp.dot(
                    user16t[which[k][t]], errors[k, t], preferred_element_type=jnp.float32
                )
            partial[f] = total.astype(jnp.bfloat16)
        for k, f in enumerate(fetches):
            for t in range(2):
                rows = pl.ds(pl.multiple_of(which[k][t] * BS, BS), BS)
                grad[rows, :] += jnp.dot(
                    errors[k, t], blocks[f], preferred_element_type=jnp.float32
                )
        return carry

    lax.fori_loop(0, GROUPS, one, 0)

    def step(b, carry):
        rows = pl.ds(b * BS, BS)
        grad[rows, :] = users[rows, :] - LEARN_RATE * grad[rows, :]
        write(b).start()
        return carry

    lax.fori_loop(0, 8, step, 0)
    for b in range(8):
        write(b).wait()


def tiles(tile_user, owner, fetch_block, users, user16, user16t, masked, fetched):
    smem, vmem, hbm = [
        pl.BlockSpec(memory_space=m) for m in (pltpu.SMEM, pltpu.VMEM, pltpu.HBM)
    ]
    held = [in_space(x, pltpu.VMEM) for x in (users, user16, user16t, masked)]
    return pl.pallas_call(
        tile_kernel,
        out_shape=(
            pltpu.HBM(users.shape, jnp.float32),
            pltpu.VMEM((FETCHES, R, BS), jnp.bfloat16),
            jax.ShapeDtypeStruct((128,), jnp.int32),
        ),
        in_specs=[smem, smem, smem, vmem, vmem, vmem, vmem, hbm],
        out_specs=[hbm, vmem, smem],
        scratch_shapes=[
            pltpu.VMEM((FETCHES, BS, R), jnp.bfloat16),
            pltpu.VMEM((GROUP, 2, BS, BS), jnp.bfloat16),
            pltpu.VMEM(users.shape, jnp.float32),
            pltpu.SemaphoreType.DMA((FETCHES,)),
            pltpu.SemaphoreType.DMA((8,)),
        ],
        compiler_params=pltpu.CompilerParams(vmem_limit_bytes=14 << 20),
        name="tile_gradients",
    )(tile_user, owner, fetch_block, *held, in_space(fetched, pltpu.HBM))


REDUCE_COPIES = 48 + 3 * (4 + 4 + 4 + 6 + 3)


def reduce_kernel(
    slots, parts, item_grad,
    outgoing0, outgoing1, outgoing2, arriving0, arriving1, arriving2, dense0, dense1, dense2,
    far0, far1, far2, near0, near1, near2, plane0, plane1, plane2, line0, line1, line2,
    row0, row1, row2, unit0, unit1, unit2, grad, send_sems, recv_sems,
):
    outgoing, arriving = (outgoing0, outgoing1, outgoing2), (arriving0, arriving1, arriving2)
    dense, far, near = (dense0, dense1, dense2), (far0, far1, far2), (near0, near1, near2)
    plane, line = (plane0, plane1, plane2), (line0, line1, line2)
    row, unit = (row0, row1, row2), (unit0, unit1, unit2)
    where = position()
    core = where[3]
    twin = sibling(where)
    net = Sender(send_sems, recv_sems)
    greeted = greet(where)
    thirds = range(3)

    def fill(target, p, parity, d3, d2):
        a1, a2, a3 = ORDERS[p]
        start, count = REDUCE_ROWS[p]

        def one(d1, carry):
            at = [None] * 3
            at[a1], at[a2], at[a3] = (
                lax.rem(where[a1] + d1, 4), lax.rem(where[a2] + d2, 4), lax.rem(where[a3] + d3, 4)
            )
            code = slots[((at[0] * 4 + at[1]) * 4 + at[2]) * 2 + parity]
            fetch = jnp.maximum(code, 0) // 2
            for block in range(2):
                low, high = max(start, block * R), min(start + count, (block + 1) * R)
                if low < high:
                    keep = (code >= 0) & (lax.rem(jnp.maximum(code, 0), 2) == block)
                    value = parts[fetch, pl.ds(low - block * R, high - low), :]
                    target[d3, d2, d1, pl.ds(low - start, high - low), :] = jnp.where(
                        keep, value, jnp.zeros_like(value)
                    )
            return carry

        lax.fori_loop(0, 4, one, 0)

    pair = {}

    def prepare(d3, d2):
        for p in thirds:
            fill(outgoing[p], p, 1 - core, d3, d2)

    def hand_over(d3, d2):
        for p in thirds:
            pair[p, d3, d2] = net.send(
                outgoing[p].at[d3, d2], arriving[p].at[d3, d2], twin
            )

    def collect(d3, d2):
        for p in thirds:
            fill(dense[p], p, core, d3, d2)
            pair[p, d3, d2].wait_recv()
            add_into(dense[p].at[d3, d2], arriving[p].at[d3, d2])

    def add_into(target, other, count=4):
        def one(n, carry):
            target[n] = (target[n].astype(jnp.float32) + other[n].astype(jnp.float32)).astype(
                jnp.bfloat16
            )
            return carry

        lax.fori_loop(0, count, one, 0)

    def add_two(target, other):
        add_into(target, other, 2)

    via = {0: 1, 1: 1, 2: -1, 3: -1}
    relay, direct = {}, {}

    def send_far(d2):
        for p in thirds:
            s = via[d2]
            relay[p, d2] = net.send(
                dense[p].at[2, d2], far[p].at[d2], shifted(where, ORDERS[p][2], s)
            )

    def send_near(d2, s):
        for p in thirds:
            if via[d2] == s:
                relay[p, d2].wait_recv()
                add_into(dense[p].at[s % 4, d2], far[p].at[d2])
            direct[p, d2, s] = net.send(
                dense[p].at[s % 4, d2],
                near[p].at[0 if s == 1 else 1, d2],
                shifted(where, ORDERS[p][2], s),
            )

    todo = [(2, 0), (2, 2), (2, 1), (2, 3), (1, 2), (3, 0), (1, 3), (3, 1)]
    todo += [(1, 0), (3, 2), (1, 1), (3, 3), (0, 0), (0, 1), (0, 2), (0, 3)]
    ahead = 2
    for d3, d2 in todo[:ahead]:
        prepare(d3, d2)
    greeted()
    for d3, d2 in todo[:ahead]:
        hand_over(d3, d2)
    for n, (d3, d2) in enumerate(todo):
        collect(d3, d2)
        if d3 == 2:
            send_far(d2)
        elif d3 != 0:
            send_near(d2, 1 if d3 == 1 else -1)
        if n + ahead < len(todo):
            prepare(*todo[n + ahead])
            hand_over(*todo[n + ahead])

    low, high = pl.ds(0, 2), pl.ds(2, 2)

    def to_line(p, name, src, dst, s):
        direct[p, name] = net.send(src, dst, shifted(where, ORDERS[p][1], s))

    for d2 in (2, 1, 3, 0):
        for p in thirds:
            for s in (1, -1):
                direct[p, d2, s].wait_recv()

            def one(n, carry, p=p, d2=d2):
                total = dense[p][0, d2, n].astype(jnp.float32)
                total += near[p][0, d2, n].astype(jnp.float32)
                total += near[p][1, d2, n].astype(jnp.float32)
                plane[p][d2, n] = total.astype(jnp.bfloat16)
                return carry

            lax.fori_loop(0, 4, one, 0)
            if d2 == 2:
                to_line(p, "far+", plane[p].at[2, low], line[p].at[2, low], 1)
                to_line(p, "far-", plane[p].at[2, high], line[p].at[2, high], -1)
            elif d2 == 1:
                to_line(p, "near+", plane[p].at[1, high], line[p].at[0, high], 1)
            elif d2 == 3:
                to_line(p, "near-", plane[p].at[3, low], line[p].at[1, low], -1)
    for p in thirds:
        direct[p, "far+"].wait_recv()
        add_two(plane[p].at[1, low], line[p].at[2, low])
        to_line(p, "last+", plane[p].at[1, low], line[p].at[0, low], 1)
        direct[p, "far-"].wait_recv()
        add_two(plane[p].at[3, high], line[p].at[2, high])
        to_line(p, "last-", plane[p].at[3, high], line[p].at[1, high], -1)
    for p in thirds:
        for name in ("near+", "near-", "last+", "last-"):
            direct[p, name].wait_recv()

        def one(n, carry, p=p):
            total = plane[p][0, n].astype(jnp.float32)
            for k in range(2):
                total += line[p][k, n].astype(jnp.float32)
            row[p][n] = total.astype(jnp.bfloat16)
            return carry

        lax.fori_loop(0, 4, one, 0)
        for d1, s in ((1, 1), (2, 2), (3, -1)):
            direct[p, "unit", s] = net.send(
                row[p].at[d1], unit[p].at[d1 - 1], shifted(where, ORDERS[p][0], s)
            )
    for p in thirds:
        start, count = REDUCE_ROWS[p]
        for s in (1, -1, 2):
            direct[p, "unit", s].wait_recv()
        total = row[p][0].astype(jnp.float32)
        for k in range(3):
            total += unit[p][k].astype(jnp.float32)
        grad[pl.ds(start, count), :] = total
    for block in range(2):
        rows = pl.ds(block * BS, BS)
        item_grad[rows, :] = grad[pl.ds(block * R, R), :].T
    net.finish()


def reduce_items(slots, partial):
    def each(*lead):
        return [pltpu.VMEM((*lead, count, BS), jnp.bfloat16) for _, count in REDUCE_ROWS]

    return pl.pallas_call(
        reduce_kernel,
        out_shape=jax.ShapeDtypeStruct((2 * BS, R), jnp.float32),
        in_specs=[
            pl.BlockSpec(memory_space=pltpu.SMEM),
            pl.BlockSpec(memory_space=pltpu.VMEM),
        ],
        out_specs=pl.BlockSpec(memory_space=pltpu.VMEM),
        scratch_shapes=[
            *each(4, 4, 4),
            *each(4, 4, 4),
            *each(4, 4, 4),
            *each(4, 4),
            *each(2, 4, 4),
            *each(4, 4),
            *each(3, 4),
            *each(4),
            *each(3),
            pltpu.VMEM((BS, BS), jnp.float32),
            pltpu.SemaphoreType.DMA((REDUCE_COPIES,)),
            pltpu.SemaphoreType.DMA((REDUCE_COPIES,)),
        ],
        compiler_params=pltpu.CompilerParams(
            collective_id=1, has_side_effects=True, vmem_limit_bytes=38 << 20
        ),
        name="reduce_items",
    )(slots, in_space(partial, pltpu.VMEM))


def body(users, items, ratings, observed, tile_user, fetch_owner, fetch_block):
    owner = fetch_owner[:, 0]
    packed = observed.reshape(FETCHES, 2, 64, 128).transpose(0, 2, 1, 3).reshape(FETCHES, 128, 128)
    gathered, masked, user16, user16t = gather(items, ratings, packed, users)
    new_users, partial, slots = tiles(
        tile_user.T, owner, fetch_block, users, user16, user16t, masked,
        gathered.reshape(256, BS, R),
    )
    new_items = items - LEARN_RATE * reduce_items(slots, partial)
    return (new_users, new_items)


def solution(mesh):
    placed = (
        P("rows", None),
        P("rows", None),
        P("rows", None, None, None),
        P("rows", None, None),
        P("rows", None),
        P("rows", None),
        P("rows"),
    )
    return jax.shard_map(
        body,
        mesh=mesh,
        in_specs=placed,
        out_specs=(P("rows", None), P("rows", None)),
        check_vma=False,
    )
```

```python
import functools

import jax
import jax.numpy as jnp
from jax import lax
from jax.experimental import pallas as pl
from jax.experimental.pallas import tpu as pltpu
from jax.sharding import PartitionSpec as P

LEARN_RATE = 0.02
MESH = pl.DeviceIdType.MESH
in_space = pltpu.with_memory_space_constraint
R = 128
BS = 256
FETCHES = 64
CHUNK = 4
STEPS = FETCHES // CHUNK
ABSENT = 1e30

ORDERS = ((2, 0, 1), (0, 1, 2), (1, 2, 0))
ROWS = ((0, 176), (176, 176), (352, 160))


def position():
    me = lax.axis_index("rows")
    return (me // 32, (me // 8) % 4, (me // 2) % 4, me % 2)


def shifted(where, axis, step):
    y, z, x, core = [
        lax.rem(w + 4 + step, 4) if a == axis else w for a, w in enumerate(where[:3])
    ] + [where[3]]
    return ((y * 4 + z) * 4 + x) * 2 + core


def sibling(where):
    y, z, x, core = where
    return ((y * 4 + z) * 4 + x) * 2 + 1 - core


def greet(where):
    barrier = pltpu.get_barrier_semaphore()
    partners = [shifted(where, a, s) for a in range(3) for s in (1, -1, 2)] + [sibling(where)]
    for partner in partners:
        pl.semaphore_signal(barrier, inc=1, device_id=(partner,), device_id_type=MESH)
    return lambda: pl.semaphore_wait(barrier, len(partners))


class Sender:
    def __init__(self, send_sems, recv_sems):
        self.send_sems, self.recv_sems, self.copies = send_sems, recv_sems, []

    def send(self, src, dst, device):
        n = len(self.copies)
        copy = pltpu.make_async_remote_copy(
            src_ref=src,
            dst_ref=dst,
            send_sem=self.send_sems.at[n],
            recv_sem=self.recv_sems.at[n],
            device_id=(device,),
            device_id_type=MESH,
        )
        copy.start()
        self.copies.append(copy)
        return copy

    def finish(self):
        for copy in self.copies:
            copy.wait_send()


GATHER_COPIES = 3 * (3 + 4 + 14 + 7) + 1 + 3 * (6 + 14 + 7)


def gather_kernel(
    items, ratings, observed, users, gathered, masked, user16, user16t,
    spread, wide_own, own, words, rate_in, obs_in, wide_users, in_sems, own_sem, user_sem, send_sems, recv_sems,
):
    where = position()
    core = where[3]
    net = Sender(send_sems, recv_sems)

    def fetch_in(n, slot):
        some = pl.ds(n * CHUNK, CHUNK)
        return (
            pltpu.make_async_copy(ratings.at[some], rate_in.at[slot], in_sems.at[0, slot]),
            pltpu.make_async_copy(observed.at[some], obs_in.at[slot], in_sems.at[1, slot]),
        )

    def one(n, carry):
        slot = lax.rem(n, 2)

        @pl.when(n + 1 < STEPS)
        def _():
            for copy in fetch_in(n + 1, 1 - slot):
                copy.start()

        for copy in fetch_in(n, slot):
            copy.wait()

        lane_group = lax.broadcasted_iota(jnp.int32, (64, 128), 1) // 32
        bit = jnp.left_shift(1, lax.broadcasted_iota(jnp.int32, (1, BS), 1) % 8)

        def fetch(k, carry):
            for t in range(2):
                packed = obs_in[slot, k, pl.ds(t, 64, stride=2), :].astype(jnp.float32)
                for quarter in range(4):
                    words[t, pl.ds(quarter, 64, stride=4), :] = jnp.where(
                        lane_group == quarter, packed, 0.0
                    )
                wide = jnp.dot(
                    words[t].astype(jnp.bfloat16), spread[...], preferred_element_type=jnp.float32
                )
                seen = (wide.astype(jnp.int32) & bit) != 0
                masked[n * CHUNK + k, t] = jnp.where(
                    seen, rate_in[slot, k, t].astype(jnp.float32), ABSENT
                ).astype(jnp.bfloat16)
            return carry

        lax.fori_loop(0, CHUNK, fetch, 0)
        return carry

    def work(first, last):
        lax.fori_loop(first, last, one, 0)

    def part(p, d1, d2, d3):
        a1, a2, a3 = ORDERS[p]
        index = [None] * 3
        index[a1], index[a2], index[a3] = d1, d2, d3
        return gathered.at[(core, *index, pl.ds(*ROWS[p]))]

    every = slice(None)
    here = gathered.at[core, 0, 0, 0]
    greeted = greet(where)
    read = pltpu.make_async_copy(items, wide_own, own_sem)
    read.start()
    read_users = pltpu.make_async_copy(users, wide_users, user_sem)
    word = lax.broadcasted_iota(jnp.int32, (128, BS), 0)
    column = lax.broadcasted_iota(jnp.int32, (128, BS), 1)
    spread[...] = jnp.where(word % 32 == column // 8, 1.0, 0.0).astype(jnp.bfloat16)
    read.wait()
    own[...] = wide_own[...].astype(jnp.bfloat16)
    place = pltpu.make_async_copy(own, here, own_sem)
    place.start()
    for copy in fetch_in(0, 0):
        copy.start()
    read_users.start()
    greeted()

    first, line, plane, pair = {}, {}, {}, []
    twin = sibling(where)

    def mirror(p, d1, d2, d3):
        pair.append(net.send(part(p, d1, d2, d3), part(p, d1, d2, d3), twin))

    thirds = range(3)
    for p in thirds:
        a1, a2, a3 = ORDERS[p]
        mine = own.at[pl.ds(*ROWS[p])]
        for s in (1, -1, 2):
            first[p, s] = net.send(mine, part(p, -s % 4, 0, 0), shifted(where, a1, s))
    for p in thirds:
        a1, a2, a3 = ORDERS[p]
        mine = own.at[pl.ds(*ROWS[p])]
        for s in (1, -1):
            plane[p, 0, s] = net.send(mine, part(p, 0, 0, -s % 4), shifted(where, a3, s))
    pair.append(net.send(own, here, twin))
    def halve(b, carry):
        value = wide_users[pl.ds(b * BS, BS), :]
        user16[b] = value.astype(jnp.bfloat16)
        user16t[b] = value.T.astype(jnp.bfloat16)
        return carry

    place.wait()
    work(0, 1)
    low, high = slice(0, 2), slice(2, 4)
    groups = {
        0: (0, 0), 1: (slice(1, 4), 0), 2: (every, 3), 3: (low, 1), 6: (high, 1),
        4: (low, 2), 5: (high, 2),
    }
    onward = {0: 1, 1: 1, 2: -1, 3: -1, 6: -1, 4: 1, 5: 1}

    def spread_group(p, g):
        a3 = ORDERS[p][2]
        d1, d2 = groups[g]
        for s in (1, -1):
            plane[p, g, s] = net.send(part(p, d1, d2, 0), part(p, d1, d2, -s % 4), shifted(where, a3, s))
        if g > 0:
            mirror(p, d1, d2, 0)

    def pass_on(g):
        for p in thirds:
            a3 = ORDERS[p][2]
            d1, d2 = groups[g]
            for s in (1, -1):
                plane[p, g, s].wait_recv()
                if onward[g] == s:
                    plane[p, g, 2] = net.send(
                        part(p, d1, d2, -s % 4), part(p, d1, d2, 2), shifted(where, a3, s)
                    )
                mirror(p, d1, d2, -s % 4)

    def passed(g):
        for p in thirds:
            plane[p, g, 2].wait_recv()
            mirror(p, *groups[g], 2)

    for p in thirds:
        a2 = ORDERS[p][1]
        for s in (1, -1, 2):
            first[p, s].wait_recv()
        for s in (1, -1):
            line[p, s] = net.send(part(p, every, 0, 0), part(p, every, -s % 4, 0), shifted(where, a2, s))
    for p in thirds:
        spread_group(p, 1)
    work(1, 2)
    pass_on(0)
    read_users.wait()
    lax.fori_loop(0, 8, halve, 0)
    work(2, 3)
    for g, s, half in ((2, 1, low), (3, -1, high)):
        for p in thirds:
            line[p, s].wait_recv()
            line[p, g + 2] = net.send(
                part(p, half, -s % 4, 0), part(p, half, 2, 0), shifted(where, ORDERS[p][1], s)
            )
            spread_group(p, g)
            if g == 3:
                spread_group(p, 6)
    work(3, 5)
    pass_on(1)
    work(5, 7)
    for g, half in ((4, low), (5, high)):
        for p in thirds:
            line[p, g].wait_recv()
            spread_group(p, g)
    work(7, 9)
    pass_on(2)
    passed(0)
    work(9, 11)
    pass_on(3)
    pass_on(6)
    passed(1)
    work(11, 13)
    pass_on(4)
    work(13, 14)
    pass_on(5)
    work(14, STEPS)
    passed(2)
    passed(4)
    passed(3)
    passed(5)
    passed(6)
    for copy in pair:
        copy.wait_recv()
    net.finish()


def gather(items, ratings, observed, users):
    return pl.pallas_call(
        gather_kernel,
        out_shape=(
            pltpu.HBM((2, 4, 4, 4, 512, R), jnp.bfloat16),
            pltpu.VMEM(ratings.shape, jnp.bfloat16),
            pltpu.VMEM((8, BS, R), jnp.bfloat16),
            pltpu.VMEM((8, R, BS), jnp.bfloat16),
        ),
        in_specs=[pl.BlockSpec(memory_space=pltpu.HBM)] * 4,
        out_specs=[pl.BlockSpec(memory_space=pltpu.HBM)]
        + [pl.BlockSpec(memory_space=pltpu.VMEM)] * 3,
        scratch_shapes=[
            pltpu.VMEM((128, BS), jnp.bfloat16),
            pltpu.VMEM((512, R), jnp.float32),
            pltpu.VMEM((512, R), jnp.bfloat16),
            pltpu.VMEM((2, BS, 128), jnp.float32),
            pltpu.VMEM((2, CHUNK, 2, BS, BS), jnp.bfloat16),
            pltpu.VMEM((2, CHUNK, 128, 128), jnp.int32),
            pltpu.VMEM(users.shape, jnp.float32),
            pltpu.SemaphoreType.DMA((2, 2)),
            pltpu.SemaphoreType.DMA,
            pltpu.SemaphoreType.DMA,
            pltpu.SemaphoreType.DMA((GATHER_COPIES,)),
            pltpu.SemaphoreType.DMA((GATHER_COPIES,)),
        ],
        compiler_params=pltpu.CompilerParams(
            collective_id=0, has_side_effects=True, vmem_limit_bytes=12 << 20
        ),
        name="gather_items",
    )(*[in_space(x, pltpu.HBM) for x in (items, ratings, observed, users)])


GROUP = 8
GROUPS = FETCHES // GROUP


def tile_kernel(
    tile_user, owner, fetch_block, users, user16, user16t, masked, fetched,
    new_users, partial, slots, blocks, errors, grad, in_sems, out_sems,
):
    where = position()

    def read(f):
        name = owner[f]
        at = (name >> 5, name >> 3, name >> 1)
        dy, dz, dx = [(a - w) & 3 for a, w in zip(at, where)]
        away = ((name & 1) << 6) + (dy << 4) + (dz << 2) + dx
        return pltpu.make_async_copy(
            fetched.at[away * 2 + fetch_block[f]], blocks.at[f], in_sems.at[f]
        )

    def write(b):
        rows = pl.ds(b * BS, BS)
        return pltpu.make_async_copy(grad.at[rows], new_users.at[rows], out_sems.at[b])

    for f in range(2 * GROUP):
        read(f).start()
    grad[...] = jnp.zeros_like(grad)

    def one(g, carry):
        @pl.when(g + 2 < GROUPS)
        def _():
            for k in range(GROUP):
                read((g + 2) * GROUP + k).start()

        @pl.when(g < GROUPS // 2)
        def _():
            for k in range(32):
                slots[g * 32 + k] = -1

        @pl.when(g >= GROUPS // 2)
        def _():
            for k in range(16):
                f = (g - GROUPS // 2) * 16 + k
                slots[owner[f]] = f * 2 + fetch_block[f]

        fetches = [g * GROUP + k for k in range(GROUP)]
        which = [[tile_user[t, f] for t in range(2)] for f in fetches]
        for f in fetches:
            pltpu.make_async_copy(fetched.at[0], blocks.at[f], in_sems.at[f]).wait()
        for k, f in enumerate(fetches):
            for t in range(2):
                predicted = lax.dot_general(
                    user16[which[k][t]], blocks[f], (((1,), (1,)), ((), ())),
                    preferred_element_type=jnp.float32,
                )
                miss = predicted - masked[f, t].astype(jnp.float32)
                errors[k, t] = jnp.where(miss > -0.5 * ABSENT, miss, 0.0).astype(jnp.bfloat16)
        for k, f in enumerate(fetches):
            total = jnp.zeros((R, BS), jnp.float32)
            for t in range(2):
                total += jnp.dot(
                    user16t[which[k][t]], errors[k, t], preferred_element_type=jnp.float32
                )
            partial[f, pl.ds(0, R), :] = total[:, :R].astype(jnp.bfloat16)
            partial[f, pl.ds(R, R), :] = total[:, R:].astype(jnp.bfloat16)
        for k, f in enumerate(fetches):
            for t in range(2):
                rows = pl.ds(pl.multiple_of(which[k][t] * BS, BS), BS)
                grad[rows, :] += jnp.dot(
                    errors[k, t], blocks[f], preferred_element_type=jnp.float32
                )
        return carry

    lax.fori_loop(0, GROUPS, one, 0)

    def step(b, carry):
        rows = pl.ds(b * BS, BS)
        grad[rows, :] = users[rows, :] - LEARN_RATE * grad[rows, :]
        write(b).start()
        return carry

    lax.fori_loop(0, 8, step, 0)
    for b in range(8):
        write(b).wait()


def tiles(tile_user, owner, fetch_block, users, user16, user16t, masked, fetched):
    smem, vmem, hbm = [
        pl.BlockSpec(memory_space=m) for m in (pltpu.SMEM, pltpu.VMEM, pltpu.HBM)
    ]
    held = [in_space(x, pltpu.VMEM) for x in (users, user16, user16t, masked)]
    return pl.pallas_call(
        tile_kernel,
        out_shape=(
            pltpu.HBM(users.shape, jnp.float32),
            pltpu.VMEM((FETCHES, BS, R), jnp.bfloat16),
            jax.ShapeDtypeStruct((128,), jnp.int32),
        ),
        in_specs=[smem, smem, smem, vmem, vmem, vmem, vmem, hbm],
        out_specs=[hbm, vmem, smem],
        scratch_shapes=[
            pltpu.VMEM((FETCHES, BS, R), jnp.bfloat16),
            pltpu.VMEM((GROUP, 2, BS, BS), jnp.bfloat16),
            pltpu.VMEM(users.shape, jnp.float32),
            pltpu.SemaphoreType.DMA((FETCHES,)),
            pltpu.SemaphoreType.DMA((8,)),
        ],
        compiler_params=pltpu.CompilerParams(vmem_limit_bytes=14 << 20),
        name="tile_gradients",
    )(tile_user, owner, fetch_block, *held, in_space(fetched, pltpu.HBM))


REDUCE_COPIES = 48 + 3 * (4 + 4 + 4 + 6 + 3)


def reduce_kernel(
    slots, parts, item_grad,
    outgoing0, outgoing1, outgoing2, arriving0, arriving1, arriving2, dense0, dense1, dense2,
    far0, far1, far2, near0, near1, near2, plane0, plane1, plane2, line0, line1, line2,
    row0, row1, row2, unit0, unit1, unit2, grad, send_sems, recv_sems,
):
    outgoing, arriving = (outgoing0, outgoing1, outgoing2), (arriving0, arriving1, arriving2)
    dense, far, near = (dense0, dense1, dense2), (far0, far1, far2), (near0, near1, near2)
    plane, line = (plane0, plane1, plane2), (line0, line1, line2)
    row, unit = (row0, row1, row2), (unit0, unit1, unit2)
    where = position()
    core = where[3]
    twin = sibling(where)
    net = Sender(send_sems, recv_sems)
    greeted = greet(where)
    thirds = range(3)

    def fill(target, p, parity, d3, d2):
        a1, a2, a3 = ORDERS[p]
        start, count = ROWS[p]

        def one(d1, carry):
            at = [None] * 3
            at[a1], at[a2], at[a3] = (
                lax.rem(where[a1] + d1, 4), lax.rem(where[a2] + d2, 4), lax.rem(where[a3] + d3, 4)
            )
            code = slots[((at[0] * 4 + at[1]) * 4 + at[2]) * 2 + parity]
            fetch = jnp.maximum(code, 0) // 2
            for block in range(2):
                low, high = max(start, block * BS), min(start + count, (block + 1) * BS)
                if low < high:
                    keep = (code >= 0) & (lax.rem(jnp.maximum(code, 0), 2) == block)
                    value = parts[fetch, pl.ds(low - block * BS, high - low), :]
                    target[d3, d2, d1, pl.ds(low - start, high - low), :] = jnp.where(
                        keep, value, jnp.zeros_like(value)
                    )
            return carry

        lax.fori_loop(0, 4, one, 0)

    pair = {}

    def prepare(d3, d2):
        for p in thirds:
            fill(outgoing[p], p, 1 - core, d3, d2)
        for p in thirds:
            fill(dense[p], p, core, d3, d2)

    def hand_over(d3, d2):
        for p in thirds:
            pair[p, d3, d2] = net.send(
                outgoing[p].at[d3, d2], arriving[p].at[d3, d2], twin
            )

    def collect(d3, d2):
        for p in thirds:
            pair[p, d3, d2].wait_recv()
            add_into(dense[p].at[d3, d2], arriving[p].at[d3, d2])

    def add_into(target, other, count=4):
        def one(n, carry):
            target[n] = (target[n].astype(jnp.float32) + other[n].astype(jnp.float32)).astype(
                jnp.bfloat16
            )
            return carry

        lax.fori_loop(0, count, one, 0)

    def add_two(target, other):
        add_into(target, other, 2)

    via = {0: 1, 1: 1, 2: -1, 3: -1}
    relay, direct = {}, {}

    def send_far(d2):
        for p in thirds:
            s = via[d2]
            relay[p, d2] = net.send(
                dense[p].at[2, d2], far[p].at[d2], shifted(where, ORDERS[p][2], s)
            )

    def send_near(d2, s):
        for p in thirds:
            if via[d2] == s:
                relay[p, d2].wait_recv()
                add_into(dense[p].at[s % 4, d2], far[p].at[d2])
            direct[p, d2, s] = net.send(
                dense[p].at[s % 4, d2],
                near[p].at[0 if s == 1 else 1, d2],
                shifted(where, ORDERS[p][2], s),
            )

    todo = [(2, 0), (2, 2), (2, 1), (2, 3), (1, 2), (3, 1), (1, 3), (3, 2)]
    todo += [(1, 1), (3, 3), (1, 0), (3, 0), (0, 2), (0, 1), (0, 3), (0, 0)]
    ahead = 3
    for d3, d2 in todo[:ahead]:
        prepare(d3, d2)
    greeted()
    for d3, d2 in todo[:ahead]:
        hand_over(d3, d2)
    for n, (d3, d2) in enumerate(todo):
        collect(d3, d2)
        if d3 == 2:
            send_far(d2)
        elif d3 != 0:
            send_near(d2, 1 if d3 == 1 else -1)
        if n + ahead < len(todo):
            prepare(*todo[n + ahead])
            hand_over(*todo[n + ahead])

    low, high = pl.ds(0, 2), pl.ds(2, 2)

    def to_line(p, name, src, dst, s):
        direct[p, name] = net.send(src, dst, shifted(where, ORDERS[p][1], s))

    for d2 in (2, 1, 3, 0):
        for p in thirds:
            for s in (1, -1):
                direct[p, d2, s].wait_recv()

            def one(n, carry, p=p, d2=d2):
                total = dense[p][0, d2, n].astype(jnp.float32)
                total += near[p][0, d2, n].astype(jnp.float32)
                total += near[p][1, d2, n].astype(jnp.float32)
                plane[p][d2, n] = total.astype(jnp.bfloat16)
                return carry

            lax.fori_loop(0, 4, one, 0)
            if d2 == 2:
                to_line(p, "far+", plane[p].at[2, low], line[p].at[2, low], 1)
                to_line(p, "far-", plane[p].at[2, high], line[p].at[2, high], -1)
            elif d2 == 1:
                to_line(p, "near+", plane[p].at[1, high], line[p].at[0, high], 1)
            elif d2 == 3:
                to_line(p, "near-", plane[p].at[3, low], line[p].at[1, low], -1)
    for p in thirds:
        direct[p, "far+"].wait_recv()
        add_two(plane[p].at[1, low], line[p].at[2, low])
        to_line(p, "last+", plane[p].at[1, low], line[p].at[0, low], 1)
        direct[p, "far-"].wait_recv()
        add_two(plane[p].at[3, high], line[p].at[2, high])
        to_line(p, "last-", plane[p].at[3, high], line[p].at[1, high], -1)
    for p in thirds:
        for name in ("near+", "near-", "last+", "last-"):
            direct[p, name].wait_recv()

        def one(n, carry, p=p):
            total = plane[p][0, n].astype(jnp.float32)
            for k in range(2):
                total += line[p][k, n].astype(jnp.float32)
            row[p][n] = total.astype(jnp.bfloat16)
            return carry

        lax.fori_loop(0, 4, one, 0)
        for d1, s in ((1, 1), (2, 2), (3, -1)):
            direct[p, "unit", s] = net.send(
                row[p].at[d1], unit[p].at[d1 - 1], shifted(where, ORDERS[p][0], s)
            )
    for p in thirds:
        start, count = ROWS[p]
        for s in (1, -1, 2):
            direct[p, "unit", s].wait_recv()
        total = row[p][0].astype(jnp.float32)
        for k in range(3):
            total += unit[p][k].astype(jnp.float32)
        grad[pl.ds(start, count), :] = total
    for quarter in range(4):
        rows = pl.ds(quarter * R, R)
        item_grad[rows, :] = grad[rows, :].T
    net.finish()


def reduce_items(slots, partial):
    def each(*lead):
        return [pltpu.VMEM((*lead, count, R), jnp.bfloat16) for _, count in ROWS]

    return pl.pallas_call(
        reduce_kernel,
        out_shape=jax.ShapeDtypeStruct((2 * BS, R), jnp.float32),
        in_specs=[
            pl.BlockSpec(memory_space=pltpu.SMEM),
            pl.BlockSpec(memory_space=pltpu.VMEM),
        ],
        out_specs=pl.BlockSpec(memory_space=pltpu.VMEM),
        scratch_shapes=[
            *each(4, 4, 4),
            *each(4, 4, 4),
            *each(4, 4, 4),
            *each(4, 4),
            *each(2, 4, 4),
            *each(4, 4),
            *each(3, 4),
            *each(4),
            *each(3),
            pltpu.VMEM((2 * BS, R), jnp.float32),
            pltpu.SemaphoreType.DMA((REDUCE_COPIES,)),
            pltpu.SemaphoreType.DMA((REDUCE_COPIES,)),
        ],
        compiler_params=pltpu.CompilerParams(
            collective_id=1, has_side_effects=True, vmem_limit_bytes=38 << 20
        ),
        name="reduce_items",
    )(slots, in_space(partial, pltpu.VMEM))


def body(users, items, ratings, observed, tile_user, fetch_owner, fetch_block):
    owner = fetch_owner[:, 0]
    packed = observed.reshape(FETCHES, 2, 64, 128).transpose(0, 2, 1, 3).reshape(FETCHES, 128, 128)
    gathered, masked, user16, user16t = gather(items, ratings, packed, users)
    new_users, partial, slots = tiles(
        tile_user.T, owner, fetch_block, users, user16, user16t, masked,
        gathered.reshape(256, BS, R),
    )
    new_items = items - LEARN_RATE * reduce_items(slots, partial)
    return (new_users, new_items)


def solution(mesh):
    placed = (
        P("rows", None),
        P("rows", None),
        P("rows", None, None, None),
        P("rows", None, None),
        P("rows", None),
        P("rows", None),
        P("rows"),
    )
    return jax.shard_map(
        body,
        mesh=mesh,
        in_specs=placed,
        out_specs=(P("rows", None), P("rows", None)),
        check_vma=False,
    )
```

```python
import functools

import jax
import jax.numpy as jnp
from jax import lax
from jax.experimental import pallas as pl
from jax.experimental.pallas import tpu as pltpu
from jax.sharding import PartitionSpec as P

LEARN_RATE = 0.02
MESH = pl.DeviceIdType.MESH
in_space = pltpu.with_memory_space_constraint
R = 128
BS = 256
FETCHES = 64
CHUNK = 4
STEPS = FETCHES // CHUNK
ABSENT = 1e30

ORDERS = ((2, 0, 1), (0, 1, 2), (1, 2, 0))
ROWS = ((0, 176), (176, 176), (352, 160))


def position():
    me = lax.axis_index("rows")
    return (me // 32, (me // 8) % 4, (me // 2) % 4, me % 2)


def shifted(where, axis, step):
    y, z, x, core = [
        lax.rem(w + 4 + step, 4) if a == axis else w for a, w in enumerate(where[:3])
    ] + [where[3]]
    return ((y * 4 + z) * 4 + x) * 2 + core


def sibling(where):
    y, z, x, core = where
    return ((y * 4 + z) * 4 + x) * 2 + 1 - core


def greet(where):
    barrier = pltpu.get_barrier_semaphore()
    partners = [shifted(where, a, s) for a in range(3) for s in (1, -1, 2)] + [sibling(where)]
    for partner in partners:
        pl.semaphore_signal(barrier, inc=1, device_id=(partner,), device_id_type=MESH)
    return lambda: pl.semaphore_wait(barrier, len(partners))


class Sender:
    def __init__(self, send_sems, recv_sems):
        self.send_sems, self.recv_sems, self.copies = send_sems, recv_sems, []

    def send(self, src, dst, device):
        n = len(self.copies)
        copy = pltpu.make_async_remote_copy(
            src_ref=src,
            dst_ref=dst,
            send_sem=self.send_sems.at[n],
            recv_sem=self.recv_sems.at[n],
            device_id=(device,),
            device_id_type=MESH,
        )
        copy.start()
        self.copies.append(copy)
        return copy

    def finish(self):
        for copy in self.copies:
            copy.wait_send()


GATHER_COPIES = 3 * (3 + 4 + 14 + 7) + 1 + 3 * (6 + 14 + 7)


def gather_kernel(
    items, ratings, observed, users, gathered, masked, user16, user16t,
    spread, wide_own, own, words, rate_in, obs_in, wide_users, in_sems, own_sem, user_sem, send_sems, recv_sems,
):
    where = position()
    core = where[3]
    net = Sender(send_sems, recv_sems)

    def fetch_in(n, slot):
        some = pl.ds(n * CHUNK, CHUNK)
        return (
            pltpu.make_async_copy(ratings.at[some], rate_in.at[slot], in_sems.at[0, slot]),
            pltpu.make_async_copy(observed.at[some], obs_in.at[slot], in_sems.at[1, slot]),
        )

    def one(n, carry):
        slot = lax.rem(n, 2)

        @pl.when(n + 1 < STEPS)
        def _():
            for copy in fetch_in(n + 1, 1 - slot):
                copy.start()

        for copy in fetch_in(n, slot):
            copy.wait()

        lane_group = lax.broadcasted_iota(jnp.int32, (64, 128), 1) // 32
        bit = jnp.left_shift(1, lax.broadcasted_iota(jnp.int32, (1, BS), 1) % 8)

        def fetch(k, carry):
            for t in range(2):
                packed = obs_in[slot, k, pl.ds(t, 64, stride=2), :].astype(jnp.float32)
                for quarter in range(4):
                    words[t, pl.ds(quarter, 64, stride=4), :] = jnp.where(
                        lane_group == quarter, packed, 0.0
                    )
                wide = jnp.dot(
                    words[t].astype(jnp.bfloat16), spread[...], preferred_element_type=jnp.float32
                )
                seen = (wide.astype(jnp.int32) & bit) != 0
                masked[n * CHUNK + k, t] = jnp.where(
                    seen, rate_in[slot, k, t].astype(jnp.float32), ABSENT
                ).astype(jnp.bfloat16)
            return carry

        lax.fori_loop(0, CHUNK, fetch, 0)
        return carry

    def work(first, last):
        lax.fori_loop(first, last, one, 0)

    def part(p, d1, d2, d3):
        a1, a2, a3 = ORDERS[p]
        index = [None] * 3
        index[a1], index[a2], index[a3] = d1, d2, d3
        return gathered.at[(core, *index, pl.ds(*ROWS[p]))]

    every = slice(None)
    here = gathered.at[core, 0, 0, 0]
    greeted = greet(where)
    read = pltpu.make_async_copy(items, wide_own, own_sem)
    read.start()
    read_users = pltpu.make_async_copy(users, wide_users, user_sem)
    word = lax.broadcasted_iota(jnp.int32, (128, BS), 0)
    column = lax.broadcasted_iota(jnp.int32, (128, BS), 1)
    spread[...] = jnp.where(word % 32 == column // 8, 1.0, 0.0).astype(jnp.bfloat16)
    read.wait()
    own[...] = wide_own[...].astype(jnp.bfloat16)
    place = pltpu.make_async_copy(own, here, own_sem)
    place.start()
    for copy in fetch_in(0, 0):
        copy.start()
    read_users.start()
    greeted()

    first, line, plane, pair = {}, {}, {}, []
    twin = sibling(where)

    def mirror(p, d1, d2, d3):
        pair.append(net.send(part(p, d1, d2, d3), part(p, d1, d2, d3), twin))

    thirds = range(3)
    for p in thirds:
        a1, a2, a3 = ORDERS[p]
        mine = own.at[pl.ds(*ROWS[p])]
        for s in (1, -1, 2):
            first[p, s] = net.send(mine, part(p, -s % 4, 0, 0), shifted(where, a1, s))
    for p in thirds:
        a1, a2, a3 = ORDERS[p]
        mine = own.at[pl.ds(*ROWS[p])]
        for s in (1, -1):
            plane[p, 0, s] = net.send(mine, part(p, 0, 0, -s % 4), shifted(where, a3, s))
    pair.append(net.send(own, here, twin))
    def halve(b, carry):
        value = wide_users[pl.ds(b * BS, BS), :]
        user16[b] = value.astype(jnp.bfloat16)
        user16t[b] = value.T.astype(jnp.bfloat16)
        return carry

    place.wait()
    work(0, 1)
    low, high = slice(0, 2), slice(2, 4)
    groups = {
        0: (0, 0), 1: (slice(1, 4), 0), 2: (every, 3), 3: (low, 1), 6: (high, 1),
        4: (low, 2), 5: (high, 2),
    }
    onward = {0: 1, 1: 1, 2: -1, 3: -1, 6: -1, 4: 1, 5: 1}

    def spread_group(p, g):
        a3 = ORDERS[p][2]
        d1, d2 = groups[g]
        for s in (1, -1):
            plane[p, g, s] = net.send(part(p, d1, d2, 0), part(p, d1, d2, -s % 4), shifted(where, a3, s))
        if g > 0:
            mirror(p, d1, d2, 0)

    def pass_on(g):
        for p in thirds:
            a3 = ORDERS[p][2]
            d1, d2 = groups[g]
            for s in (1, -1):
                plane[p, g, s].wait_recv()
                if onward[g] == s:
                    plane[p, g, 2] = net.send(
                        part(p, d1, d2, -s % 4), part(p, d1, d2, 2), shifted(where, a3, s)
                    )
                mirror(p, d1, d2, -s % 4)

    def passed(g):
        for p in thirds:
            plane[p, g, 2].wait_recv()
            mirror(p, *groups[g], 2)

    for p in thirds:
        a2 = ORDERS[p][1]
        for s in (1, -1, 2):
            first[p, s].wait_recv()
        for s in (1, -1):
            line[p, s] = net.send(part(p, every, 0, 0), part(p, every, -s % 4, 0), shifted(where, a2, s))
    for p in thirds:
        spread_group(p, 1)
    work(1, 2)
    pass_on(0)
    read_users.wait()
    lax.fori_loop(0, 8, halve, 0)
    work(2, 3)
    for g, s, half in ((2, 1, low), (3, -1, high)):
        for p in thirds:
            line[p, s].wait_recv()
            line[p, g + 2] = net.send(
                part(p, half, -s % 4, 0), part(p, half, 2, 0), shifted(where, ORDERS[p][1], s)
            )
            spread_group(p, g)
            if g == 3:
                spread_group(p, 6)
    work(3, 5)
    pass_on(1)
    work(5, 7)
    for g, half in ((4, low), (5, high)):
        for p in thirds:
            line[p, g].wait_recv()
            spread_group(p, g)
    work(7, 9)
    pass_on(2)
    passed(0)
    work(9, 11)
    pass_on(3)
    pass_on(6)
    passed(1)
    work(11, 13)
    pass_on(4)
    work(13, 14)
    pass_on(5)
    work(14, STEPS)
    passed(2)
    passed(4)
    passed(3)
    passed(5)
    passed(6)
    for copy in pair:
        copy.wait_recv()
    net.finish()


def gather(items, ratings, observed, users):
    return pl.pallas_call(
        gather_kernel,
        out_shape=(
            pltpu.VMEM((2, 4, 4, 4, 512, R), jnp.bfloat16),
            pltpu.VMEM(ratings.shape, jnp.bfloat16),
            pltpu.VMEM((8, BS, R), jnp.bfloat16),
            pltpu.VMEM((8, R, BS), jnp.bfloat16),
        ),
        in_specs=[pl.BlockSpec(memory_space=pltpu.HBM)] * 4,
        out_specs=[pl.BlockSpec(memory_space=pltpu.VMEM)] * 4,
        scratch_shapes=[
            pltpu.VMEM((128, BS), jnp.bfloat16),
            pltpu.VMEM((512, R), jnp.float32),
            pltpu.VMEM((512, R), jnp.bfloat16),
            pltpu.VMEM((2, BS, 128), jnp.float32),
            pltpu.VMEM((2, CHUNK, 2, BS, BS), jnp.bfloat16),
            pltpu.VMEM((2, CHUNK, 128, 128), jnp.int32),
            pltpu.VMEM(users.shape, jnp.float32),
            pltpu.SemaphoreType.DMA((2, 2)),
            pltpu.SemaphoreType.DMA,
            pltpu.SemaphoreType.DMA,
            pltpu.SemaphoreType.DMA((GATHER_COPIES,)),
            pltpu.SemaphoreType.DMA((GATHER_COPIES,)),
        ],
        compiler_params=pltpu.CompilerParams(
            collective_id=0, has_side_effects=True, vmem_limit_bytes=7 << 20
        ),
        name="gather_items",
    )(*[in_space(x, pltpu.HBM) for x in (items, ratings, observed, users)])


GROUP = 8
GROUPS = FETCHES // GROUP


def tile_kernel(
    tile_user, owner, fetch_block, users, user16, user16t, masked, fetched,
    new_users, partial, slots, errors, grad, out_sems,
):
    where = position()

    def item(f):
        name = owner[f]
        at = (name >> 5, name >> 3, name >> 1)
        dy, dz, dx = [(a - w) & 3 for a, w in zip(at, where)]
        rows = pl.ds(pl.multiple_of(fetch_block[f] * BS, BS), BS)
        return fetched.at[name & 1, dy, dz, dx, rows]

    def write(b):
        rows = pl.ds(b * BS, BS)
        return pltpu.make_async_copy(grad.at[rows], new_users.at[rows], out_sems.at[b])

    grad[...] = jnp.zeros_like(grad)

    def one(g, carry):
        @pl.when(g < GROUPS // 2)
        def _():
            for k in range(32):
                slots[g * 32 + k] = -1

        @pl.when(g >= GROUPS // 2)
        def _():
            for k in range(16):
                f = (g - GROUPS // 2) * 16 + k
                slots[owner[f]] = f * 2 + fetch_block[f]

        fetches = [g * GROUP + k for k in range(GROUP)]
        which = [[tile_user[t, f] for t in range(2)] for f in fetches]
        blocks = [item(f) for f in fetches]
        for k, f in enumerate(fetches):
            for t in range(2):
                predicted = lax.dot_general(
                    user16[which[k][t]], blocks[k][...], (((1,), (1,)), ((), ())),
                    preferred_element_type=jnp.float32,
                )
                miss = predicted - masked[f, t].astype(jnp.float32)
                errors[k, t] = jnp.where(miss > -0.5 * ABSENT, miss, 0.0).astype(jnp.bfloat16)
        for k, f in enumerate(fetches):
            total = jnp.zeros((R, BS), jnp.float32)
            for t in range(2):
                total += jnp.dot(
                    user16t[which[k][t]], errors[k, t], preferred_element_type=jnp.float32
                )
            partial[f, pl.ds(0, R), :] = total[:, :R].astype(jnp.bfloat16)
            partial[f, pl.ds(R, R), :] = total[:, R:].astype(jnp.bfloat16)
            for t in range(2):
                rows = pl.ds(pl.multiple_of(which[k][t] * BS, BS), BS)
                grad[rows, :] += jnp.dot(
                    errors[k, t], blocks[k][...], preferred_element_type=jnp.float32
                )
        return carry

    lax.fori_loop(0, GROUPS, one, 0)

    def step(b, carry):
        rows = pl.ds(b * BS, BS)
        grad[rows, :] = users[rows, :] - LEARN_RATE * grad[rows, :]
        write(b).start()
        return carry

    lax.fori_loop(0, 8, step, 0)
    for b in range(8):
        write(b).wait()


def tiles(tile_user, owner, fetch_block, users, user16, user16t, masked, fetched):
    smem, vmem, hbm = [
        pl.BlockSpec(memory_space=m) for m in (pltpu.SMEM, pltpu.VMEM, pltpu.HBM)
    ]
    held = [in_space(x, pltpu.VMEM) for x in (users, user16, user16t, masked, fetched)]
    return pl.pallas_call(
        tile_kernel,
        out_shape=(
            pltpu.HBM(users.shape, jnp.float32),
            pltpu.VMEM((FETCHES, BS, R), jnp.bfloat16),
            jax.ShapeDtypeStruct((128,), jnp.int32),
        ),
        in_specs=[smem, smem, smem, vmem, vmem, vmem, vmem, vmem],
        out_specs=[hbm, vmem, smem],
        scratch_shapes=[
            pltpu.VMEM((GROUP, 2, BS, BS), jnp.bfloat16),
            pltpu.VMEM(users.shape, jnp.float32),
            pltpu.SemaphoreType.DMA((8,)),
        ],
        compiler_params=pltpu.CompilerParams(vmem_limit_bytes=6 << 20),
        name="tile_gradients",
    )(tile_user, owner, fetch_block, *held)


REDUCE_COPIES = 48 + 3 * (4 + 4 + 4 + 6 + 3)


def reduce_kernel(
    slots, parts, item_grad,
    outgoing0, outgoing1, outgoing2, arriving0, arriving1, arriving2, dense0, dense1, dense2,
    far0, far1, far2, near0, near1, near2, plane0, plane1, plane2, line0, line1, line2,
    row0, row1, row2, unit0, unit1, unit2, grad, send_sems, recv_sems,
):
    outgoing, arriving = (outgoing0, outgoing1, outgoing2), (arriving0, arriving1, arriving2)
    dense, far, near = (dense0, dense1, dense2), (far0, far1, far2), (near0, near1, near2)
    plane, line = (plane0, plane1, plane2), (line0, line1, line2)
    row, unit = (row0, row1, row2), (unit0, unit1, unit2)
    where = position()
    core = where[3]
    twin = sibling(where)
    net = Sender(send_sems, recv_sems)
    greeted = greet(where)
    thirds = range(3)

    def fill(target, p, parity, d3, d2):
        a1, a2, a3 = ORDERS[p]
        start, count = ROWS[p]

        def one(d1, carry):
            at = [None] * 3
            at[a1], at[a2], at[a3] = (
                lax.rem(where[a1] + d1, 4), lax.rem(where[a2] + d2, 4), lax.rem(where[a3] + d3, 4)
            )
            code = slots[((at[0] * 4 + at[1]) * 4 + at[2]) * 2 + parity]
            fetch = jnp.maximum(code, 0) // 2
            for block in range(2):
                low, high = max(start, block * BS), min(start + count, (block + 1) * BS)
                if low < high:
                    keep = (code >= 0) & (lax.rem(jnp.maximum(code, 0), 2) == block)
                    value = parts[fetch, pl.ds(low - block * BS, high - low), :]
                    target[d3, d2, d1, pl.ds(low - start, high - low), :] = jnp.where(
                        keep, value, jnp.zeros_like(value)
                    )
            return carry

        lax.fori_loop(0, 4, one, 0)

    pair = {}

    def prepare(d3, d2):
        for p in thirds:
            fill(outgoing[p], p, 1 - core, d3, d2)

    def fill_own(d3, d2):
        for p in thirds:
            fill(dense[p], p, core, d3, d2)

    def hand_over(d3, d2):
        for p in thirds:
            pair[p, d3, d2] = net.send(
                outgoing[p].at[d3, d2], arriving[p].at[d3, d2], twin
            )

    def collect(d3, d2):
        for p in thirds:
            pair[p, d3, d2].wait_recv()
            add_into(dense[p].at[d3, d2], arriving[p].at[d3, d2])

    def add_into(target, other, count=4):
        def one(n, carry):
            target[n] = (target[n].astype(jnp.float32) + other[n].astype(jnp.float32)).astype(
                jnp.bfloat16
            )
            return carry

        lax.fori_loop(0, count, one, 0)

    def add_two(target, other):
        add_into(target, other, 2)

    via = {0: 1, 1: 1, 2: -1, 3: -1}
    relay, direct = {}, {}

    def send_far(d2):
        for p in thirds:
            s = via[d2]
            relay[p, d2] = net.send(
                dense[p].at[2, d2], far[p].at[d2], shifted(where, ORDERS[p][2], s)
            )

    def send_near(d2, s):
        for p in thirds:
            if via[d2] == s:
                relay[p, d2].wait_recv()
                add_into(dense[p].at[s % 4, d2], far[p].at[d2])
            direct[p, d2, s] = net.send(
                dense[p].at[s % 4, d2],
                near[p].at[0 if s == 1 else 1, d2],
                shifted(where, ORDERS[p][2], s),
            )

    todo = [(2, 0), (2, 2), (2, 1), (2, 3), (1, 2), (3, 1), (1, 3), (3, 2)]
    todo += [(1, 1), (3, 3), (1, 0), (3, 0), (0, 2), (0, 1), (0, 3), (0, 0)]
    ahead = 3
    prepare(*todo[0])
    greeted()
    hand_over(*todo[0])
    prepare(*todo[1])
    hand_over(*todo[1])
    for n, (d3, d2) in enumerate(todo):
        fill_own(d3, d2)
        collect(d3, d2)
        if d3 == 2:
            send_far(d2)
        elif d3 != 0:
            send_near(d2, 1 if d3 == 1 else -1)
        for item in todo[2 if n == 0 else n + ahead : n + ahead + 1]:
            prepare(*item)
            hand_over(*item)

    low, high = pl.ds(0, 2), pl.ds(2, 2)

    def to_line(p, name, src, dst, s):
        direct[p, name] = net.send(src, dst, shifted(where, ORDERS[p][1], s))

    for d2 in (2, 1, 3, 0):
        for p in thirds:
            for s in (1, -1):
                direct[p, d2, s].wait_recv()

            def one(n, carry, p=p, d2=d2):
                total = dense[p][0, d2, n].astype(jnp.float32)
                total += near[p][0, d2, n].astype(jnp.float32)
                total += near[p][1, d2, n].astype(jnp.float32)
                plane[p][d2, n] = total.astype(jnp.bfloat16)
                return carry

            lax.fori_loop(0, 4, one, 0)
            if d2 == 2:
                to_line(p, "far+", plane[p].at[2, low], line[p].at[2, low], 1)
                to_line(p, "far-", plane[p].at[2, high], line[p].at[2, high], -1)
            elif d2 == 1:
                to_line(p, "near+", plane[p].at[1, high], line[p].at[0, high], 1)
            elif d2 == 3:
                to_line(p, "near-", plane[p].at[3, low], line[p].at[1, low], -1)
    for p in thirds:
        direct[p, "far+"].wait_recv()
        add_two(plane[p].at[1, low], line[p].at[2, low])
        to_line(p, "last+", plane[p].at[1, low], line[p].at[0, low], 1)
        direct[p, "far-"].wait_recv()
        add_two(plane[p].at[3, high], line[p].at[2, high])
        to_line(p, "last-", plane[p].at[3, high], line[p].at[1, high], -1)
    for p in thirds:
        for name in ("near+", "near-", "last+", "last-"):
            direct[p, name].wait_recv()

        def one(n, carry, p=p):
            total = plane[p][0, n].astype(jnp.float32)
            for k in range(2):
                total += line[p][k, n].astype(jnp.float32)
            row[p][n] = total.astype(jnp.bfloat16)
            return carry

        lax.fori_loop(0, 4, one, 0)
        for d1, s in ((1, 1), (2, 2), (3, -1)):
            direct[p, "unit", s] = net.send(
                row[p].at[d1], unit[p].at[d1 - 1], shifted(where, ORDERS[p][0], s)
            )
    for p in thirds:
        start, count = ROWS[p]
        for s in (1, -1, 2):
            direct[p, "unit", s].wait_recv()
        total = row[p][0].astype(jnp.float32)
        for k in range(3):
            total += unit[p][k].astype(jnp.float32)
        grad[pl.ds(start, count), :] = total
    for quarter in range(4):
        rows = pl.ds(quarter * R, R)
        item_grad[rows, :] = grad[rows, :].T
    net.finish()


def reduce_items(slots, partial):
    def each(*lead):
        return [pltpu.VMEM((*lead, count, R), jnp.bfloat16) for _, count in ROWS]

    return pl.pallas_call(
        reduce_kernel,
        out_shape=jax.ShapeDtypeStruct((2 * BS, R), jnp.float32),
        in_specs=[
            pl.BlockSpec(memory_space=pltpu.SMEM),
            pl.BlockSpec(memory_space=pltpu.VMEM),
        ],
        out_specs=pl.BlockSpec(memory_space=pltpu.VMEM),
        scratch_shapes=[
            *each(4, 4, 4),
            *each(4, 4, 4),
            *each(4, 4, 4),
            *each(4, 4),
            *each(2, 4, 4),
            *each(4, 4),
            *each(3, 4),
            *each(4),
            *each(3),
            pltpu.VMEM((2 * BS, R), jnp.float32),
            pltpu.SemaphoreType.DMA((REDUCE_COPIES,)),
            pltpu.SemaphoreType.DMA((REDUCE_COPIES,)),
        ],
        compiler_params=pltpu.CompilerParams(
            collective_id=1, has_side_effects=True, vmem_limit_bytes=38 << 20
        ),
        name="reduce_items",
    )(slots, in_space(partial, pltpu.VMEM))


def body(users, items, ratings, observed, tile_user, fetch_owner, fetch_block):
    owner = fetch_owner[:, 0]
    packed = observed.reshape(FETCHES, 2, 64, 128).transpose(0, 2, 1, 3).reshape(FETCHES, 128, 128)
    gathered, masked, user16, user16t = gather(items, ratings, packed, users)
    new_users, partial, slots = tiles(
        tile_user.T, owner, fetch_block, users, user16, user16t, masked, gathered
    )
    new_items = items - LEARN_RATE * reduce_items(slots, partial)
    return (new_users, new_items)


def solution(mesh):
    placed = (
        P("rows", None),
        P("rows", None),
        P("rows", None, None, None),
        P("rows", None, None),
        P("rows", None),
        P("rows", None),
        P("rows"),
    )
    return jax.shard_map(
        body,
        mesh=mesh,
        in_specs=placed,
        out_specs=(P("rows", None), P("rows", None)),
        check_vma=False,
    )
```
